32 devices in a mesh: dp: 4 (over x, core), blk: 4 (over z), head: 2 (over y).
Axes of the slice: x: 2, y: 2, z: 4, core: 2. Of those that a mesh axis runs over, the one named last changes fastest.
Arguments:
- block_input: bfloat16 [4, 1024, 1280], P('dp', ('blk', 'head')), may hold values from -6 to 6
- block_ids: int32 [4, 1024], P('dp', 'blk'), may hold values from 0 to 7, never falling along the last dimension, each value on 1 to 256 neighbouring positions
- w_qkv: bfloat16 [1280, 3840], P(('dp', 'blk', 'head')), may hold values from -0.15625 to 0.15625
- w_out: bfloat16 [1280, 1280], P(('dp', 'blk', 'head')), may hold values from -1 to 1
- w_up: bfloat16 [1280, 1280], P(('dp', 'blk', 'head')), may hold values from -0.15625 to 0.15625
- w_down: bfloat16 [1280, 1280], P(('dp', 'blk', 'head')), may hold values from -0.15625 to 0.15625
- gain_attn: bfloat16 [1280], P(('dp', 'blk', 'head')), may hold values from 0.5 to 1.5
- gain_mlp: bfloat16 [1280], P(('dp', 'blk', 'head')), may hold values from 0.5 to 1.5
- bias_up: bfloat16 [1280], P(('dp', 'blk', 'head')), may hold values from -3 to 3
- bias_down: bfloat16 [1280], P(('dp', 'blk', 'head')), may hold values from -1.75 to 1.75
- query_scale: float32 [80], replicated, may hold values from -0.5 to 1.5
- out_cotangent: bfloat16 [4, 1024, 1280], P('dp', ('blk', 'head')), may hold values from -6 to 6
Outputs:
- output: bfloat16 [4, 1024, 1280], P('dp', ('blk', 'head'))
- grad_input: float32 [4, 1024, 1280], P('dp', ('blk', 'head'))
- grad_w_qkv: float32 [1280, 3840], P(('dp', 'blk', 'head'))
- grad_w_out: float32 [1280, 1280], P(('dp', 'blk', 'head'))
- grad_w_up: float32 [1280, 1280], P(('dp', 'blk', 'head'))
- grad_w_down: float32 [1280, 1280], P(('dp', 'blk', 'head'))
- grad_gain_attn: float32 [1280], P(('dp', 'blk', 'head'))
- grad_gain_mlp: float32 [1280], P(('dp', 'blk', 'head'))
- grad_bias_up: float32 [1280], P(('dp', 'blk', 'head'))
- grad_bias_down: float32 [1280], P(('dp', 'blk', 'head'))
- grad_query_scale: float32 [80], replicated
The draws below stay inside these ranges and needn't reach their ends.
Inputs may be any that keep to these rules, and one draw needn't show every extreme that they name: `block_ids`: block numbers never fall along a sequence and start at 0; each block holds 1 to 256 tokens, and some block holds exactly 256.
All inputs are finite; a program needn't handle non-finite values.
Results may differ from the reference program's by a relative error of at most 0.03.
Values may be sent and summed in bfloat16 or wider, within the bound.
No kernel may reach another device: no remote copies, remote signals or barrier semaphores. Data moves between devices by JAX's collectives and lax.ppermute only.
A program may use at most 256 MiB of HBM per device.

```python
import math
from functools import partial
import jax
import jax.numpy as jnp
import numpy as np
from jax import lax

D = 1280
HEADS = 16
HEAD_DIM = 80
FF = 1280
BLOCK = 256
SEQ = 1024
SEQS = 4


def shard_levels(key, extent, shards, low, high):
    def one(axis_at, parts):
        heights = jax.random.uniform(jax.random.fold_in(jax.random.fold_in(key, 6), axis_at), (parts,), jnp.float32, low / len(shards), high / len(shards))
        return jnp.repeat(jnp.exp(heights), extent[axis_at] // parts).reshape((-1,) + (1,) * (len(extent) - axis_at - 1))

    level = one(*shards[0])
    for cut in shards[1:]:
        level = level * one(*cut)
    return level


def length_profile(amount, total, bound, slope):
    weights = [(1 << 20) // math.isqrt(grade ** slope) + 1 for grade in range(2, amount + 1)]
    surplus, given = total - bound - (amount - 1), [1] * (amount - 1)
    while surplus > 0:
        candidates = [i for i in range(amount - 1) if given[i] < bound]
        whole, left = sum([weights[i] for i in candidates]), surplus
        for i in candidates:
            extra = min(bound - given[i], max(1, left * weights[i] // whole), surplus)
            given[i] = given[i] + extra
            surplus = surplus - extra
    return np.array([bound] + given)


def uneven(own_key, amount, total, reach, lean):
    if amount == 2:
        one = jax.random.randint(own_key, (), max(1, total - reach), min(reach, total - 1) + 1)
        return jnp.stack([one, total - one])
    lengths = jnp.asarray(length_profile(amount, total, reach, lean), jnp.int32)
    twos = (amount - 1) // 2
    source_of, receiver = lengths[1:1 + 2 * twos:2], lengths[2:2 + 2 * twos:2]
    room = jnp.minimum(source_of - 1, reach - receiver)
    shifted = jax.random.randint(jax.random.fold_in(own_key, 1), (twos,), 0, 1 << 20) % (room + 1)
    lengths = lengths.at[1:1 + 2 * twos:2].set(source_of - shifted).at[2:2 + 2 * twos:2].set(receiver + shifted)
    return lengths[jax.random.permutation(jax.random.fold_in(own_key, 2), amount)]


def noise(key, shape, deviation, limit, shards=(), kind=jnp.bfloat16):
    factor_of = shard_levels(key, shape, shards, -0.22, 0.18) if shards else 1.0
    values = jax.random.normal(key, shape, jnp.float32) * deviation * factor_of
    return jnp.minimum(jnp.maximum(values, -limit), limit).astype(kind)


def setup_inputs(seed: int = 0) -> dict:
    splits = jax.random.split(jax.random.key(seed), 13)
    return {
        "block_input": noise(splits[0], (SEQS, SEQ, D), 1.0, 6.0, ((0, 4), (1, 8))),
        "block_ids": jax.vmap(lambda own: jnp.searchsorted(jnp.cumsum(uneven(own, 2 * SEQ // BLOCK, SEQ, BLOCK, 0)), jnp.arange(SEQ), side="right"))(jax.random.split(splits[1], SEQS)).reshape((SEQS, SEQ)).astype(jnp.int32),
        "w_qkv": noise(splits[2], (D, 3 * D), D ** -0.5, 0.15625, ((0, 32),)),
        "w_out": noise(splits[3], (D, D), (max(1, D * 32 // SEQ)) ** -0.5, 1.0, ((0, 32),)),
        "w_up": noise(splits[4], (D, FF), D ** -0.5, 0.15625, ((0, 32),)),
        "w_down": noise(splits[5], (FF, D), FF ** -0.5, 0.15625, ((0, 32),)),
        "gain_attn": jnp.clip(1.0 + 0.1 * jax.random.normal(splits[6], (D,), jnp.float32), 0.5, 1.5).astype(jnp.bfloat16),
        "gain_mlp": jnp.clip(1.0 + 0.1 * jax.random.normal(splits[7], (D,), jnp.float32), 0.5, 1.5).astype(jnp.bfloat16),
        "bias_up": noise(splits[8], (FF,), 0.5, 3.0, ((0, 32),)),
        "bias_down": noise(splits[9], (D,), 0.3, 1.75, ((0, 32),)),
        "query_scale": jnp.clip(jax.random.uniform(splits[10], (HEAD_DIM,), jnp.float32, -0.5, 1.5), -0.5, 1.5),
        "out_cotangent": noise(splits[11], (SEQS, SEQ, D), 1.0, 6.0, ((0, 4), (1, 8))),
    }


norm_eps = 1e-06
scale_base = 1.442695041

@jax.custom_vjp
def low(v):
    return lax.optimization_barrier(v.astype(jnp.bfloat16)).astype(jnp.float32)

@jax.custom_vjp
def low_back(v):
    return v

def low_keep(v):
    return (low(v), None)

def low_pass(kept, grad):
    return (grad,)

def back_keep(v):
    return (v, None)

def back_low(kept, grad):
    return (low(grad),)
low.defvjp(low_keep, low_pass)
low_back.defvjp(back_keep, back_low)

def rms(values_in, gain):
    return values_in * lax.rsqrt(lax.optimization_barrier(jnp.mean(values_in * values_in, axis=-1, keepdims=True)) + norm_eps) * gain

def matmul(left, right):
    return jnp.einsum('...d,de->...e', left, right, precision=lax.Precision.HIGHEST)

def one_block(query_rows, row_ids, key_all, value_all, key_ids):
    scores = jnp.einsum('qhd,khd->hqk', query_rows, key_all, precision=lax.Precision.HIGHEST)
    scores = low_back(scores)
    allowed = key_ids[None, :] <= row_ids[:, None]
    scores = jnp.where(allowed[None], scores, -1e+30)
    probs = low(jax.nn.softmax(scores, axis=-1))
    return jnp.einsum('hqk,khd->qhd', probs, value_all, precision=lax.Precision.HIGHEST)

def attend(queries, keys, values, block_ids):
    query_block = min(512, SEQ)
    block_count = SEQ // query_block
    checked = jax.checkpoint(one_block)

    def per_sequence(items):
        seq_queries, seq_keys, seq_values, seq_ids = items
        key_all = seq_keys.reshape(SEQ, HEADS, HEAD_DIM)
        value_all = seq_values.reshape(SEQ, HEADS, HEAD_DIM)
        query_blocks = seq_queries.reshape(block_count, query_block, HEADS, HEAD_DIM)
        id_blocks = seq_ids.reshape(block_count, query_block)

        def per_block(pair):
            return checked(pair[0], pair[1], key_all, value_all, seq_ids)
        result = lax.map(per_block, (query_blocks, id_blocks))
        return result.reshape(SEQ, D)
    return lax.map(per_sequence, (queries, keys, values, block_ids))

def forward(block_ids, block_input, w_qkv, w_out, w_up, w_down, gain_attn, gain_mlp, bias_up, bias_down, query_scale):
    h_first = low(rms(block_input, gain_attn))
    qkv = matmul(h_first, w_qkv)
    q_raw = low_back(qkv[..., :D])
    keys = low(low_back(qkv[..., D:2 * D]))
    values = low(low_back(qkv[..., 2 * D:]))
    factor = jnp.tile(scale_base / math.sqrt(HEAD_DIM) * jax.nn.softplus(query_scale), HEADS)
    queries = low(low_back(q_raw * factor))
    attn = low(low_back(attend(queries, keys, values, block_ids)))
    mixed = block_input + low_back(matmul(attn, w_out))
    h_second = low(rms(mixed, gain_mlp))
    pre_act = low_back(matmul(h_second, w_up) + bias_up)
    act = low(jax.nn.silu(pre_act))
    return mixed + matmul(act, w_down) + bias_down

def reference(block_input, block_ids, w_qkv, w_out, w_up, w_down, gain_attn, gain_mlp, bias_up, bias_down, query_scale, out_cotangent):
    floats = [block_input, w_qkv, w_out, w_up, w_down, gain_attn, gain_mlp, bias_up, bias_down, query_scale]
    floats = [item.astype(jnp.float32) for item in floats]
    layer = partial(forward, block_ids)
    result, pull_back = jax.vjp(layer, floats[0], floats[1], floats[2], floats[3], floats[4], floats[5], floats[6], floats[7], floats[8], floats[9])
    grads = pull_back(out_cotangent.astype(jnp.float32))
    return (result.astype(jnp.bfloat16), grads[0], grads[1], grads[2], grads[3], grads[4], grads[5], grads[6], grads[7], grads[8], grads[9])
```

```python
from functools import partial
import math

import jax
import jax.numpy as jnp
from jax import lax
from jax.sharding import PartitionSpec as P

HEADS = 16
HEAD_DIM = 80


norm_eps = 1e-06
scale_base = 1.442695041


def rms_fwd(values_in, gain):
    inverse = lax.rsqrt(jnp.mean(values_in * values_in, axis=-1, keepdims=True) + norm_eps)
    return (values_in * inverse * gain, inverse)


def rms_back(incoming, values_in, inverse, gain):
    normed = values_in * inverse
    gain_grad = jnp.sum(incoming * normed, axis=0)
    scaled = incoming * gain
    input_grad = inverse * (scaled - normed * jnp.mean(scaled * normed, axis=-1, keepdims=True))
    return (gain_grad, input_grad)


def block_rows_of(row_count):
    return math.gcd(row_count, 512)


def sweep_rows(step_fn, running, pieces):
    row_count = pieces[0].shape[0]
    block_rows = block_rows_of(row_count)
    block_count = row_count // block_rows

    def turn_body(turn_index, current):
        sub_piece = tuple(
            (
                lax.dynamic_slice_in_dim(array_in, turn_index * block_rows, block_rows, 0)
                for array_in in pieces
            )
        )
        return step_fn(current, sub_piece)

    return lax.fori_loop(0, block_count, turn_body, running)


def split_heads(rows_in, head_count):
    return rows_in.reshape(rows_in.shape[0], head_count, -1)


def attend_step(query_heads, query_ids, running, sub_piece):
    maxima, totals, weighted = running
    key_rows, value_rows, key_ids = sub_piece
    key_heads = split_heads(key_rows, query_heads.shape[1])
    value_heads = split_heads(value_rows, query_heads.shape[1])
    scores = jnp.einsum("rhd,khd->hrk", query_heads, key_heads, preferred_element_type=jnp.float32)
    allowed = (key_ids[None, :] <= query_ids[:, None])[None]
    scores = jnp.where(allowed, scores, -1e30)
    new_max = jnp.maximum(maxima, jnp.max(scores, axis=-1))
    rescale = jnp.exp(maxima - new_max)
    weights = jnp.where(allowed, jnp.exp(scores - new_max[..., None]), 0.0)
    totals = totals * rescale + jnp.sum(weights, axis=-1)
    weighted = weighted * rescale[..., None] + jnp.einsum(
        "hrk,khd->hrd",
        weights.astype(jnp.bfloat16),
        value_heads,
        preferred_element_type=jnp.float32,
    )
    return (new_max, totals, weighted)


def probabilities(
    query_heads, grad_heads, log_sums, deltas, query_ids, key_heads, value_heads, key_ids
):
    scores = jnp.einsum("rhd,khd->hrk", query_heads, key_heads, preferred_element_type=jnp.float32)
    allowed = (key_ids[None, :] <= query_ids[:, None])[None]
    scores = jnp.where(allowed, scores, -1e30)
    probs = jnp.where(allowed, jnp.exp(scores - log_sums[..., None]), 0.0)
    grad_probs = jnp.einsum(
        "rhd,khd->hrk", grad_heads, value_heads, preferred_element_type=jnp.float32
    )
    grad_scores = probs * (grad_probs - deltas[..., None])
    return (probs.astype(jnp.bfloat16), grad_scores.astype(jnp.bfloat16))


def shards(
    block_input,
    block_ids,
    w_qkv,
    w_out,
    w_up,
    w_down,
    gain_attn,
    gain_mlp,
    bias_up,
    bias_down,
    query_scale,
    out_cotangent,
):
    gathered = (
        lax.all_gather(w_qkv, ("dp", "blk", "head"), axis=0, tiled=True),
        lax.all_gather(w_out, ("dp", "blk", "head"), axis=0, tiled=True),
        lax.all_gather(w_up, ("dp", "blk", "head"), axis=0, tiled=True),
        lax.all_gather(w_down, ("dp", "blk", "head"), axis=0, tiled=True),
        lax.all_gather(gain_attn, ("dp", "blk", "head"), axis=0, tiled=True),
        lax.all_gather(gain_mlp, ("dp", "blk", "head"), axis=0, tiled=True),
        lax.all_gather(bias_up, ("dp", "blk", "head"), axis=0, tiled=True),
        lax.all_gather(bias_down, ("dp", "blk", "head"), axis=0, tiled=True),
    )
    full_qkv, full_out, full_up, full_down = (gathered[0], gathered[1], gathered[2], gathered[3])
    gain_one = gathered[4].astype(jnp.float32)
    gain_two = gathered[5].astype(jnp.float32)
    up_bias = gathered[6].astype(jnp.float32)
    down_bias = gathered[7].astype(jnp.float32)
    width = block_input.shape[2]
    local_heads = HEADS // lax.axis_size("head")
    x_rows = block_input[0].astype(jnp.float32)
    query_ids = block_ids[0]
    normed_one, inverse_one = rms_fwd(x_rows, gain_one)
    h_first = normed_one.astype(jnp.bfloat16)
    qkv = jnp.dot(h_first, full_qkv, preferred_element_type=jnp.float32)
    q_raw = qkv[:, :width]
    factor = jnp.tile(scale_base / math.sqrt(HEAD_DIM) * jax.nn.softplus(query_scale), HEADS)
    q_scaled = (q_raw * factor).astype(jnp.bfloat16)
    key_low = qkv[:, width : 2 * width].astype(jnp.bfloat16)
    value_low = qkv[:, 2 * width :].astype(jnp.bfloat16)
    query_rows, key_rows, value_rows = (
        lax.all_to_all(q_scaled, "head", split_axis=1, concat_axis=0, tiled=True),
        lax.all_to_all(key_low, "head", split_axis=1, concat_axis=0, tiled=True),
        lax.all_to_all(value_low, "head", split_axis=1, concat_axis=0, tiled=True),
    )
    row_count = query_rows.shape[0]
    query_heads = split_heads(query_rows, local_heads)
    start_state = (
        jnp.full((local_heads, row_count), -1e30, jnp.float32),
        jnp.zeros((local_heads, row_count), jnp.float32),
        jnp.zeros((local_heads, row_count, HEAD_DIM), jnp.float32),
    )
    maxima, totals, weighted = sweep_rows(
        partial(attend_step, query_heads, query_ids),
        start_state,
        (
            lax.all_gather(key_rows, "blk", axis=0, tiled=True),
            lax.all_gather(value_rows, "blk", axis=0, tiled=True),
            lax.all_gather(query_ids, "blk", axis=0, tiled=True),
        ),
    )
    log_sums = maxima + jnp.log(totals)
    attention = weighted / totals[..., None]
    attn_rows = jnp.transpose(attention, (1, 0, 2)).reshape(row_count, -1).astype(jnp.bfloat16)
    merged = lax.all_to_all(attn_rows, "head", split_axis=0, concat_axis=1, tiled=True)
    mixed = x_rows + jnp.dot(merged, full_out, preferred_element_type=jnp.float32)
    normed_two, inverse_two = rms_fwd(mixed, gain_two)
    h_second = normed_two.astype(jnp.bfloat16)
    pre_act = jnp.dot(h_second, full_up, preferred_element_type=jnp.float32) + up_bias
    act_low = jax.nn.silu(pre_act).astype(jnp.bfloat16)
    result = mixed + jnp.dot(act_low, full_down, preferred_element_type=jnp.float32) + down_bias
    cot_rows = out_cotangent[0]
    cot_float = cot_rows.astype(jnp.float32)
    grad_bdown = jnp.sum(cot_float, axis=0)
    grad_act = jnp.einsum("td,fd->tf", cot_rows, full_down, preferred_element_type=jnp.float32)
    sigmoid_pre = jax.nn.sigmoid(pre_act)
    grad_pre = (grad_act * sigmoid_pre * (1.0 + pre_act * (1.0 - sigmoid_pre))).astype(jnp.bfloat16)
    grad_bup = jnp.sum(grad_pre.astype(jnp.float32), axis=0)
    grad_h_second = jnp.einsum("tf,df->td", grad_pre, full_up, preferred_element_type=jnp.float32)
    grad_gain_two, grad_mixed_norm = rms_back(grad_h_second, mixed, inverse_two, gain_two)
    grad_mixed = cot_float + grad_mixed_norm
    branch_grad = grad_mixed.astype(jnp.bfloat16)
    grad_merged = jnp.einsum(
        "td,ed->te", branch_grad, full_out, preferred_element_type=jnp.float32
    ).astype(jnp.bfloat16)
    grad_rows = lax.all_to_all(grad_merged, "head", split_axis=1, concat_axis=0, tiled=True)
    grad_heads = split_heads(grad_rows, local_heads)
    deltas = jnp.einsum("rhd,hrd->hr", grad_heads.astype(jnp.float32), attention)
    whole_keys, whole_values, whole_ids = (
        lax.all_gather(key_rows, "blk", axis=0, tiled=True),
        lax.all_gather(value_rows, "blk", axis=0, tiled=True),
        lax.all_gather(query_ids, "blk", axis=0, tiled=True),
    )
    total_rows = whole_keys.shape[0]
    block_rows = block_rows_of(total_rows)
    block_count = total_rows // block_rows

    def key_step(grad_query_sum, block_piece):
        key_block, value_block, id_block = block_piece
        key_heads = split_heads(key_block, local_heads)
        value_heads = split_heads(value_block, local_heads)
        probs_low, grad_scores = probabilities(
            query_heads, grad_heads, log_sums, deltas, query_ids, key_heads, value_heads, id_block
        )
        grad_query_sum = grad_query_sum + jnp.einsum(
            "hrk,khd->hrd", grad_scores, key_heads, preferred_element_type=jnp.float32
        )
        key_term = jnp.einsum(
            "hrk,rhd->khd", grad_scores, query_heads, preferred_element_type=jnp.float32
        ).reshape(block_rows, -1)
        value_term = jnp.einsum(
            "hrk,rhd->khd", probs_low, grad_heads, preferred_element_type=jnp.float32
        ).reshape(block_rows, -1)
        return (grad_query_sum, jnp.stack((key_term, value_term), axis=1))

    grad_query_acc, key_terms = lax.scan(
        key_step,
        jnp.zeros((local_heads, row_count, HEAD_DIM), jnp.float32),
        (
            whole_keys.reshape(block_count, block_rows, -1),
            whole_values.reshape(block_count, block_rows, -1),
            whole_ids.reshape(block_count, block_rows),
        ),
    )
    summed = lax.psum_scatter(
        key_terms.reshape(total_rows, 2, -1).astype(jnp.bfloat16),
        "blk",
        scatter_dimension=0,
        tiled=True,
    ).astype(jnp.float32)
    grad_key_rows = summed[:, 0]
    grad_value_rows = summed[:, 1]
    grad_query_rows = (
        jnp.transpose(grad_query_acc, (1, 0, 2)).reshape(row_count, -1).astype(jnp.bfloat16)
    )
    back_query, back_key, back_value = (
        lax.all_to_all(grad_query_rows, "head", split_axis=0, concat_axis=1, tiled=True),
        lax.all_to_all(
            grad_key_rows.astype(jnp.bfloat16), "head", split_axis=0, concat_axis=1, tiled=True
        ),
        lax.all_to_all(
            grad_value_rows.astype(jnp.bfloat16), "head", split_axis=0, concat_axis=1, tiled=True
        ),
    )
    grad_q_scaled = back_query.astype(jnp.float32)
    scale_terms = jnp.sum(grad_q_scaled * q_raw, axis=0).reshape(HEADS, HEAD_DIM).sum(axis=0)
    scale_local = scale_terms * (scale_base / math.sqrt(HEAD_DIM)) * jax.nn.sigmoid(query_scale)
    grad_q_raw = (grad_q_scaled * factor).astype(jnp.bfloat16)
    grad_qkv_rows = jnp.concatenate([grad_q_raw, back_key, back_value], axis=1)
    grad_h_first = jnp.einsum(
        "te,de->td", grad_qkv_rows, full_qkv, preferred_element_type=jnp.float32
    )
    grad_gain_one, grad_x_norm = rms_back(grad_h_first, x_rows, inverse_one, gain_one)
    grad_x = grad_mixed + grad_x_norm
    term_qkv = jnp.einsum("tr,te->re", h_first, grad_qkv_rows, preferred_element_type=jnp.float32)
    term_out = jnp.einsum("tr,te->re", merged, branch_grad, preferred_element_type=jnp.float32)
    term_up = jnp.einsum("tr,te->re", h_second, grad_pre, preferred_element_type=jnp.float32)
    term_down = jnp.einsum("tr,te->re", act_low, cot_rows, preferred_element_type=jnp.float32)
    stacked = lax.psum_scatter(
        jnp.concatenate([term_qkv, term_out, term_up, term_down], axis=1),
        ("dp", "blk", "head"),
        scatter_dimension=0,
        tiled=True,
    )
    shares = (
        lax.psum_scatter(grad_gain_one, ("dp", "blk", "head"), scatter_dimension=0, tiled=True),
        lax.psum_scatter(grad_gain_two, ("dp", "blk", "head"), scatter_dimension=0, tiled=True),
        lax.psum_scatter(grad_bup, ("dp", "blk", "head"), scatter_dimension=0, tiled=True),
        lax.psum_scatter(grad_bdown, ("dp", "blk", "head"), scatter_dimension=0, tiled=True),
    )
    scale_total = lax.psum(scale_local, ("dp", "blk", "head"))
    share_qkv = stacked[:, : 3 * width]
    share_out = stacked[:, 3 * width : 4 * width]
    share_up = stacked[:, 4 * width : 5 * width]
    share_down = stacked[:, 5 * width :]
    return (
        result.astype(jnp.bfloat16)[None],
        grad_x[None],
        share_qkv,
        share_out,
        share_up,
        share_down,
        shares[0],
        shares[1],
        shares[2],
        shares[3],
        scale_total,
    )


BIT_X, BIT_C, BIT_Z1, BIT_Z0, BIT_Y = 16, 8, 4, 2, 1
AXES = ("dp", "blk", "head")
BF = jnp.bfloat16
F32 = jnp.float32


def flip(array, mask_even, mask_odd):
    pairs = [(i, i ^ (mask_odd if i & BIT_C else mask_even)) for i in range(32)]
    return lax.ppermute(array, AXES, pairs)


def flip_core(array):
    return flip(array, BIT_C, BIT_C)


def turn(array):
    def other(i):
        c, z1 = (i // BIT_C) & 1, (i // BIT_Z1) & 1
        return (i & ~(BIT_C | BIT_Z1)) | (z1 * BIT_C) | (c * BIT_Z1)
    return lax.ppermute(array, AXES, [(i, other(i)) for i in range(32)])


def dot(a, b, dims):
    return lax.dot_general(a, b, (dims, ((), ())), preferred_element_type=F32)


def place(blocks, index_of, axis=0):
    out = jnp.zeros((len(blocks),) + blocks[0].shape, blocks[0].dtype)
    for d, block in enumerate(blocks):
        out = lax.dynamic_update_index_in_dim(out, block, index_of(d), 0)
    return out


def square_shards(block_input, block_ids, w_qkv, w_out, w_up, w_down, gain_attn, gain_mlp,
                  bias_up, bias_down, query_scale, out_cotangent):
    width = block_input.shape[2]
    tok = block_input.shape[1]
    shard = w_qkv.shape[0]
    me = lax.axis_index(AXES)
    bit_x, bit_c, bit_z1, bit_z0, bit_y = [(me // b) & 1 for b in (16, 8, 4, 2, 1)]
    core = bit_c == 1
    j = me & 3
    first = jnp.where(core, BIT_Z0, BIT_Y)
    second = 3 - first
    disp = (0, first, second, 3)
    flip_first = lambda a: flip(a, BIT_Y, BIT_Z0)
    flip_second = lambda a: flip(a, BIT_Z0, BIT_Y)

    ids_own = lax.dynamic_slice_in_dim(block_ids[0], bit_y * tok, tok, 0)
    x_ids = jnp.concatenate(
        [block_input[0], jnp.broadcast_to(ids_own.astype(BF)[:, None], (tok, 128))], axis=1)
    x_ids = turn(x_ids)
    x_low = x_ids[:, :width]
    x_rows = x_low.astype(F32)

    g_one = gain_attn.astype(F32)
    wq = (w_qkv.astype(F32) * g_one[:, None]).astype(BF)
    wq = wq.reshape(shard, 3, 2, 2, 2, 2 * HEAD_DIM).transpose(3, 2, 4, 0, 1, 5).reshape(
        2, 4, shard, 6 * HEAD_DIM)
    wq_keep = jnp.where(core, wq[1], wq[0])
    wq_sib = flip_core(jnp.where(core, wq[0], wq[1]))
    pair = jnp.stack([wq_keep, wq_sib], axis=1)
    rel = [lax.dynamic_index_in_dim(pair, j ^ d, 0, keepdims=False) for d in disp]
    got = flip_first(jnp.stack([rel[1], rel[3]]))
    got2 = flip_second(jnp.stack([rel[2], got[1]]))
    blocks = [rel[0], got[0], got2[0], got2[1]]
    grid = place(blocks, lambda d: j ^ disp[d])
    grid = jnp.where(core, grid[:, ::-1], grid).transpose(1, 0, 2, 3).reshape(
        2, 4 * shard, 6 * HEAD_DIM)
    a1 = flip(grid, BIT_X, BIT_Z1)
    a2 = flip(jnp.stack([grid, a1]), BIT_Z1, BIT_X)
    k_now = bit_x * 2 + bit_z1
    d_first = jnp.where(core, 1, 2)
    wq_full = place([grid, a1, a2[0], a2[1]], lambda d: k_now ^ (0, d_first, 3 - d_first, 3)[d])
    wq_full = wq_full.reshape(2, 2, 2, 4 * shard, 6 * HEAD_DIM).transpose(0, 2, 1, 3, 4).reshape(
        width, 6 * HEAD_DIM)

    g_two = gain_mlp.astype(F32)
    up_scaled = (w_up.astype(F32) * g_two[:, None]).astype(BF)
    up_parts = up_scaled.reshape(shard, 2, 2, width // 4)
    up_keep = jnp.where(core, up_parts[:, :, 1], up_parts[:, :, 0]).reshape(shard, width // 2)
    up_send = jnp.where(core, up_parts[:, :, 0], up_parts[:, :, 1]).reshape(shard, width // 2)
    up_sib = flip_core(up_send)
    extra = jnp.stack([bias_up, bias_down], axis=1)
    extra = jnp.pad(extra, ((0, 0), (0, 126)))
    pay = jnp.concatenate([w_out, up_keep, up_sib, w_down, extra], axis=1)
    b1 = flip(pay, BIT_Z1, BIT_Z0)
    b2 = flip(jnp.stack([pay, b1]), BIT_Z0, BIT_Z1)
    k_z = bit_z1 * 2 + bit_z0
    z_first = jnp.where(core, 1, 2)
    zgrid = place([pay, b1, b2[0], b2[1]], lambda d: k_z ^ (0, z_first, 3 - z_first, 3)[d])
    b3 = flip(zgrid, BIT_Y, BIT_X)
    b4 = flip(jnp.stack([zgrid, b3]), BIT_X, BIT_Y)
    k_xy = bit_x * 2 + bit_y
    xy_first = jnp.where(core, 2, 1)
    full = place([zgrid, b3, b4[0], b4[1]], lambda d: k_xy ^ (0, xy_first, 3 - xy_first, 3)[d])
    half = width // 2
    full = full.reshape(2, 2, 4, shard, pay.shape[1]).transpose(0, 2, 1, 3, 4).reshape(half, -1)
    wo = full[:, :width]
    wup_own = full[:, width : width + half]
    wup_sib = full[:, width + half : 2 * width]
    wdn = full[:, 2 * width : 3 * width]
    b_up = full[:, 3 * width].astype(F32)
    b_dn_own = full[:, 3 * width + 1]
    b_dn_sib = flip_core(b_dn_own)

    def both_cores(own, sib):
        own = own.reshape(own.shape[:-1] + (2, half // 2))
        sib = sib.reshape(sib.shape[:-1] + (2, half // 2))
        pairs = jnp.where(core, jnp.stack([sib, own], axis=-2), jnp.stack([own, sib], axis=-2))
        return pairs.reshape(pairs.shape[:-3] + (width,))

    def own_columns(rows):
        parts = rows.reshape(rows.shape[0], 2, 2, half // 2)
        return jnp.where(core, parts[:, :, 1], parts[:, :, 0]).reshape(rows.shape[0], half)

    def sib_columns(rows):
        parts = rows.reshape(rows.shape[0], 2, 2, half // 2)
        return jnp.where(core, parts[:, :, 0], parts[:, :, 1]).reshape(rows.shape[0], half)

    b_dn = both_cores(b_dn_own, b_dn_sib).astype(F32)
    wo_groups = wo.reshape(4, half // 4, width)
    wo_rel = jnp.concatenate(
        [lax.dynamic_index_in_dim(wo_groups, j ^ d, 0, keepdims=False) for d in disp], axis=0)

    inv_one = lax.rsqrt(jnp.mean(x_rows * x_rows, axis=-1, keepdims=True) + norm_eps)
    n_one = (x_rows * inv_one).astype(BF)
    n_msg = jnp.concatenate([n_one, x_ids[:, width:]], axis=1)
    r1 = flip_first(n_msg)
    r2 = flip_second(jnp.concatenate([n_msg, r1], axis=0))
    m0, m1, m2 = flip_core(n_msg), flip_core(r1), flip_core(r2)
    tokens = jnp.concatenate(
        [n_msg, m0, r1, m2[:tok], r2[:tok], m1, r2[tok:], m2[tok:]], axis=0)
    n_all = tokens[:, :width]
    ids_all = tokens[:, width]
    cot_own = turn(out_cotangent[0])
    cot_sib = flip_core(cot_own)
    cot_pair = jnp.concatenate([cot_own, cot_sib], axis=0)

    qkv = dot(n_all, wq_full, ((1,), (0,)))
    hw = 2 * HEAD_DIM
    q_raw = qkv[:, :hw]
    factor1 = scale_base / math.sqrt(HEAD_DIM) * jax.nn.softplus(query_scale)
    factor = jnp.tile(factor1, 2)
    q_h = (q_raw * factor).astype(BF).reshape(-1, 2, HEAD_DIM)
    k_h = qkv[:, hw : 2 * hw].astype(BF).reshape(-1, 2, HEAD_DIM)
    v_h = qkv[:, 2 * hw :].astype(BF).reshape(-1, 2, HEAD_DIM)
    scores = jnp.einsum("rhd,khd->hrk", q_h, k_h, preferred_element_type=F32)
    allowed = (ids_all[None, :] <= ids_all[:, None])[None]
    scores = jnp.where(allowed, scores, -1e30)
    top = jnp.max(scores, axis=-1, keepdims=True)
    weights = jnp.where(allowed, jnp.exp(scores - top), 0.0)
    probs = weights / jnp.sum(weights, axis=-1, keepdims=True)
    probs_low = probs.astype(BF)
    attn = jnp.einsum("hrk,khd->rhd", probs_low, v_h, preferred_element_type=F32)
    attn = attn.reshape(4, 2 * tok, hw).astype(BF)

    s1 = flip_first(jnp.stack([attn[1], attn[3]]))
    s2 = flip_second(jnp.stack([attn[2], s1[1]]))
    merged = jnp.concatenate([attn[0], s1[0], s2[0], s2[1]], axis=1)

    def share(partial_rows):
        return partial_rows[:tok] + flip_core(partial_rows[tok:].astype(BF)).astype(F32)

    x2 = x_rows + share(dot(merged, wo_rel, ((1,), (0,))))
    inv_two = lax.rsqrt(jnp.mean(x2 * x2, axis=-1, keepdims=True) + norm_eps)
    norm_two = x2 * inv_two
    n_two = norm_two.astype(BF)
    n_pair = jnp.concatenate([n_two, flip_core(n_two)], axis=0)
    n_pair_own, n_pair_sib = own_columns(n_pair), sib_columns(n_pair)
    u = dot(n_pair_own, wup_own, ((1,), (0,))) + dot(n_pair_sib, wup_sib, ((1,), (0,))) + b_up
    sig = jax.nn.sigmoid(u)
    act = (u * sig).astype(BF)
    out = x2 + share(dot(act, wdn, ((1,), (0,)))) + b_dn
    out = turn(out.astype(BF))
    d_act = dot(cot_pair, wdn, ((1,), (1,)))
    d_pre = (d_act * sig * (1.0 + u * (1.0 - sig))).astype(BF)
    d_n_own = dot(d_pre, wup_own, ((1,), (1,)))
    d_n_sib = dot(d_pre, wup_sib, ((1,), (1,)))
    d_n_two = share(both_cores(d_n_own, d_n_sib))
    mean_two = jnp.mean(d_n_two * norm_two, axis=-1, keepdims=True)
    d_x2 = cot_own.astype(F32) + inv_two * (d_n_two - norm_two * mean_two)
    d_branch = d_x2.astype(BF)
    d_branch_pair = jnp.concatenate([d_branch, flip_core(d_branch)], axis=0)
    d_attn = dot(d_branch_pair, wo_rel, ((1,), (1,))).astype(BF)
    da = [d_attn[:, d * hw : (d + 1) * hw] for d in range(4)]
    e = flip_second(jnp.stack([da[2], da[3]]))
    t = flip_first(jnp.stack([da[1], e[1]]))
    d_o = jnp.concatenate([da[0], t[0], e[0], t[1]], axis=0).reshape(-1, 2, HEAD_DIM)

    d_p = jnp.einsum("rhd,khd->hrk", d_o, v_h, preferred_element_type=F32)
    delta = jnp.sum(probs * d_p, axis=-1, keepdims=True)
    d_s = (probs * (d_p - delta)).astype(BF)
    d_q = jnp.einsum("hrk,khd->rhd", d_s, k_h, preferred_element_type=F32).reshape(-1, hw).astype(BF)
    d_k = jnp.einsum("hrk,rhd->khd", d_s, q_h, preferred_element_type=F32).reshape(-1, hw).astype(BF)
    d_v = jnp.einsum("hrk,rhd->khd", probs_low, d_o, preferred_element_type=F32).reshape(-1, hw).astype(BF)
    d_q32 = d_q.astype(F32)
    scale_part = jnp.sum(d_q32 * q_raw, axis=0)
    scale_part = scale_part[:HEAD_DIM] + scale_part[HEAD_DIM:]
    scale_part = scale_part * (scale_base / math.sqrt(HEAD_DIM)) * jax.nn.sigmoid(query_scale)
    d_qkv = jnp.concatenate([(d_q32 * factor).astype(BF), d_k, d_v], axis=1)

    d_n = dot(d_qkv, wq_full, ((1,), (1,))).reshape(4, 2, tok, width)
    from_sib = flip_core(d_n[:, 1].astype(BF)).astype(F32)
    td = [d_n[0, 0] + from_sib[0], d_n[1, 0] + from_sib[2], d_n[2, 0] + from_sib[1], d_n[3, 0] + from_sib[3]]
    p1 = flip_second(jnp.stack([td[2], td[3]]).astype(BF)).astype(F32)
    p2 = flip_first((td[1] + p1[1]).astype(BF)).astype(F32)
    d_n_one = td[0] + p1[0] + p2
    norm_one = x_rows * inv_one
    mean_one = jnp.mean(d_n_one * norm_one, axis=-1, keepdims=True)
    grad_x = d_x2 + inv_one * (d_n_one - norm_one * mean_one)
    grad_x = turn(grad_x.astype(BF)).astype(F32)

    g_out_rel = dot(merged, d_branch_pair, ((0,), (0,))).astype(BF).reshape(4, half // 4, width)
    g_out = place([g_out_rel[d] for d in range(4)], lambda d: j ^ disp[d]).reshape(half, width)
    g_up_own = dot(n_pair_own, d_pre, ((0,), (0,))).astype(BF)
    g_up_sib = dot(n_pair_sib, d_pre, ((0,), (0,))).astype(BF)
    g_dn = dot(act, cot_pair, ((0,), (0,))).astype(BF)
    s_up = jnp.sum(d_pre.astype(F32), axis=0)
    s_dn = jnp.sum(own_columns(cot_pair).astype(F32), axis=0)
    g_extra = jnp.pad(jnp.stack([s_up, s_dn], axis=1), ((0, 0), (0, 126))).astype(BF)
    g = jnp.concatenate([g_out, g_up_own, g_up_sib, g_dn, g_extra], axis=1)
    g = g.reshape(2, 4, 2, shard, -1).transpose(0, 2, 1, 3, 4).reshape(4, 4, shard, -1)
    pick = lambda a, i: lax.dynamic_index_in_dim(a, i, 0, keepdims=False)
    xd = jnp.where(core, 1, 2)
    q1 = flip(jnp.stack([pick(g, k_xy ^ xd), pick(g, k_xy ^ 3)]), BIT_X, BIT_Y).astype(F32)
    q2 = flip((pick(g, k_xy ^ (3 - xd)).astype(F32) + q1[1]).astype(BF), BIT_Y, BIT_X).astype(F32)
    gz = pick(g, k_xy).astype(F32) + q1[0] + q2
    zd = jnp.where(core, 2, 1)
    zd = jnp.where(core, 2, 1)
    q3 = flip(jnp.stack([pick(gz, k_z ^ zd), pick(gz, k_z ^ 3)]).astype(BF), BIT_Z0, BIT_Z1).astype(F32)
    q4 = flip((pick(gz, k_z ^ (3 - zd)) + q3[1]).astype(BF), BIT_Z1, BIT_Z0).astype(F32)
    mine = pick(gz, k_z) + q3[0] + q4
    share_out = mine[:, :width]
    up_half = mine[:, width : width + half]
    up_other = flip_core(mine[:, width + half : 2 * width].astype(BF)).astype(F32)
    raw_up = both_cores(up_half, up_other)
    share_up = raw_up * g_two[:, None]
    grad_gain_two = jnp.sum(raw_up * w_up.astype(F32), axis=1)
    share_down = mine[:, 2 * width : 3 * width]
    grad_bup = mine[:, 3 * width]
    grad_bdown = mine[:, 3 * width + 1]

    g_qkv = dot(n_all, d_qkv, ((0,), (0,)))
    scale_cols = jnp.pad(scale_part, (0, 128 - HEAD_DIM))
    g_qkv = jnp.concatenate([g_qkv, jnp.broadcast_to(scale_cols, (width, 128))], axis=1).astype(BF)
    wide = g_qkv.shape[1]
    g_qkv = g_qkv.reshape(2, 2, 2, 4 * shard, wide).transpose(0, 2, 1, 3, 4).reshape(
        4, 2, 4 * shard, wide)
    qd = jnp.where(core, 2, 1)
    v1 = flip(jnp.stack([pick(g_qkv, k_now ^ qd), pick(g_qkv, k_now ^ 3)]), BIT_Z1, BIT_X).astype(F32)
    v2 = flip((pick(g_qkv, k_now ^ (3 - qd)).astype(F32) + v1[1]).astype(BF), BIT_X, BIT_Z1).astype(F32)
    gq = (pick(g_qkv, k_now).astype(F32) + v1[0] + v2).astype(BF)
    gq = gq.reshape(2, 4, shard, wide)
    keep, send = jnp.where(core, gq[1], gq[0]), jnp.where(core, gq[0], gq[1])
    pairs = jnp.stack([keep, flip_core(send)], axis=1)
    rel = [lax.dynamic_index_in_dim(pairs, j ^ d, 0, keepdims=False) for d in disp]
    got = flip_first(jnp.stack([rel[1], rel[3]]))
    got2 = flip_second(jnp.stack([rel[2], got[1]]))
    grid = place([rel[0], got[0], got2[0], got2[1]], lambda d: j ^ disp[d])
    grid = jnp.where(core, grid[:, ::-1], grid)
    scale_total = jnp.sum(grid[:, :, 0, 6 * HEAD_DIM :].astype(F32), axis=(0, 1))[:HEAD_DIM]
    raw_qkv = grid[..., : 6 * HEAD_DIM].reshape(2, 2, 2, shard, 3, hw)
    raw_qkv = raw_qkv.transpose(3, 4, 0, 2, 1, 5).reshape(shard, 3 * width).astype(F32)
    share_qkv = raw_qkv * g_one[:, None]
    grad_gain_one = jnp.sum(raw_qkv * w_qkv.astype(F32), axis=1)
    return (out[None], grad_x[None], share_qkv, share_out, share_up, share_down,
            grad_gain_one, grad_gain_two, grad_bup, grad_bdown, scale_total)


def solution(mesh):
    placed = (
        P("dp", ("blk", "head"), None),
        P("dp", "blk"),
        P(("dp", "blk", "head"), None),
        P(("dp", "blk", "head"), None),
        P(("dp", "blk", "head"), None),
        P(("dp", "blk", "head"), None),
        P(("dp", "blk", "head")),
        P(("dp", "blk", "head")),
        P(("dp", "blk", "head")),
        P(("dp", "blk", "head")),
        P(),
        P("dp", ("blk", "head"), None),
    )
    square = dict(mesh.shape) == {"dp": 4, "blk": 4, "head": 2}
    return jax.shard_map(
        square_shards if square else shards,
        mesh=mesh,
        in_specs=placed,
        out_specs=(
            P("dp", ("blk", "head"), None),
            P("dp", ("blk", "head"), None),
            P(("dp", "blk", "head"), None),
            P(("dp", "blk", "head"), None),
            P(("dp", "blk", "head"), None),
            P(("dp", "blk", "head"), None),
            P(("dp", "blk", "head")),
            P(("dp", "blk", "head")),
            P(("dp", "blk", "head")),
            P(("dp", "blk", "head")),
            P(),
        ),
        check_vma=False,
    )
```

```python
from functools import partial
import math

import jax
import jax.numpy as jnp
from jax import lax
from jax.experimental import pallas as pl
from jax.experimental.pallas import tpu as pltpu
from jax.sharding import PartitionSpec as P

HEADS = 16
HEAD_DIM = 80


norm_eps = 1e-06
scale_base = 1.442695041


def rms_fwd(values_in, gain):
    inverse = lax.rsqrt(jnp.mean(values_in * values_in, axis=-1, keepdims=True) + norm_eps)
    return (values_in * inverse * gain, inverse)


def rms_back(incoming, values_in, inverse, gain):
    normed = values_in * inverse
    gain_grad = jnp.sum(incoming * normed, axis=0)
    scaled = incoming * gain
    input_grad = inverse * (scaled - normed * jnp.mean(scaled * normed, axis=-1, keepdims=True))
    return (gain_grad, input_grad)


def block_rows_of(row_count):
    return math.gcd(row_count, 512)


def sweep_rows(step_fn, running, pieces):
    row_count = pieces[0].shape[0]
    block_rows = block_rows_of(row_count)
    block_count = row_count // block_rows

    def turn_body(turn_index, current):
        sub_piece = tuple(
            (
                lax.dynamic_slice_in_dim(array_in, turn_index * block_rows, block_rows, 0)
                for array_in in pieces
            )
        )
        return step_fn(current, sub_piece)

    return lax.fori_loop(0, block_count, turn_body, running)


def split_heads(rows_in, head_count):
    return rows_in.reshape(rows_in.shape[0], head_count, -1)


def attend_step(query_heads, query_ids, running, sub_piece):
    maxima, totals, weighted = running
    key_rows, value_rows, key_ids = sub_piece
    key_heads = split_heads(key_rows, query_heads.shape[1])
    value_heads = split_heads(value_rows, query_heads.shape[1])
    scores = jnp.einsum("rhd,khd->hrk", query_heads, key_heads, preferred_element_type=jnp.float32)
    allowed = (key_ids[None, :] <= query_ids[:, None])[None]
    scores = jnp.where(allowed, scores, -1e30)
    new_max = jnp.maximum(maxima, jnp.max(scores, axis=-1))
    rescale = jnp.exp(maxima - new_max)
    weights = jnp.where(allowed, jnp.exp(scores - new_max[..., None]), 0.0)
    totals = totals * rescale + jnp.sum(weights, axis=-1)
    weighted = weighted * rescale[..., None] + jnp.einsum(
        "hrk,khd->hrd",
        weights.astype(jnp.bfloat16),
        value_heads,
        preferred_element_type=jnp.float32,
    )
    return (new_max, totals, weighted)


def probabilities(
    query_heads, grad_heads, log_sums, deltas, query_ids, key_heads, value_heads, key_ids
):
    scores = jnp.einsum("rhd,khd->hrk", query_heads, key_heads, preferred_element_type=jnp.float32)
    allowed = (key_ids[None, :] <= query_ids[:, None])[None]
    scores = jnp.where(allowed, scores, -1e30)
    probs = jnp.where(allowed, jnp.exp(scores - log_sums[..., None]), 0.0)
    grad_probs = jnp.einsum(
        "rhd,khd->hrk", grad_heads, value_heads, preferred_element_type=jnp.float32
    )
    grad_scores = probs * (grad_probs - deltas[..., None])
    return (probs.astype(jnp.bfloat16), grad_scores.astype(jnp.bfloat16))


def shards(
    block_input,
    block_ids,
    w_qkv,
    w_out,
    w_up,
    w_down,
    gain_attn,
    gain_mlp,
    bias_up,
    bias_down,
    query_scale,
    out_cotangent,
):
    gathered = (
        lax.all_gather(w_qkv, ("dp", "blk", "head"), axis=0, tiled=True),
        lax.all_gather(w_out, ("dp", "blk", "head"), axis=0, tiled=True),
        lax.all_gather(w_up, ("dp", "blk", "head"), axis=0, tiled=True),
        lax.all_gather(w_down, ("dp", "blk", "head"), axis=0, tiled=True),
        lax.all_gather(gain_attn, ("dp", "blk", "head"), axis=0, tiled=True),
        lax.all_gather(gain_mlp, ("dp", "blk", "head"), axis=0, tiled=True),
        lax.all_gather(bias_up, ("dp", "blk", "head"), axis=0, tiled=True),
        lax.all_gather(bias_down, ("dp", "blk", "head"), axis=0, tiled=True),
    )
    full_qkv, full_out, full_up, full_down = (gathered[0], gathered[1], gathered[2], gathered[3])
    gain_one = gathered[4].astype(jnp.float32)
    gain_two = gathered[5].astype(jnp.float32)
    up_bias = gathered[6].astype(jnp.float32)
    down_bias = gathered[7].astype(jnp.float32)
    width = block_input.shape[2]
    local_heads = HEADS // lax.axis_size("head")
    x_rows = block_input[0].astype(jnp.float32)
    query_ids = block_ids[0]
    normed_one, inverse_one = rms_fwd(x_rows, gain_one)
    h_first = normed_one.astype(jnp.bfloat16)
    qkv = jnp.dot(h_first, full_qkv, preferred_element_type=jnp.float32)
    q_raw = qkv[:, :width]
    factor = jnp.tile(scale_base / math.sqrt(HEAD_DIM) * jax.nn.softplus(query_scale), HEADS)
    q_scaled = (q_raw * factor).astype(jnp.bfloat16)
    key_low = qkv[:, width : 2 * width].astype(jnp.bfloat16)
    value_low = qkv[:, 2 * width :].astype(jnp.bfloat16)
    query_rows, key_rows, value_rows = (
        lax.all_to_all(q_scaled, "head", split_axis=1, concat_axis=0, tiled=True),
        lax.all_to_all(key_low, "head", split_axis=1, concat_axis=0, tiled=True),
        lax.all_to_all(value_low, "head", split_axis=1, concat_axis=0, tiled=True),
    )
    row_count = query_rows.shape[0]
    query_heads = split_heads(query_rows, local_heads)
    start_state = (
        jnp.full((local_heads, row_count), -1e30, jnp.float32),
        jnp.zeros((local_heads, row_count), jnp.float32),
        jnp.zeros((local_heads, row_count, HEAD_DIM), jnp.float32),
    )
    maxima, totals, weighted = sweep_rows(
        partial(attend_step, query_heads, query_ids),
        start_state,
        (
            lax.all_gather(key_rows, "blk", axis=0, tiled=True),
            lax.all_gather(value_rows, "blk", axis=0, tiled=True),
            lax.all_gather(query_ids, "blk", axis=0, tiled=True),
        ),
    )
    log_sums = maxima + jnp.log(totals)
    attention = weighted / totals[..., None]
    attn_rows = jnp.transpose(attention, (1, 0, 2)).reshape(row_count, -1).astype(jnp.bfloat16)
    merged = lax.all_to_all(attn_rows, "head", split_axis=0, concat_axis=1, tiled=True)
    mixed = x_rows + jnp.dot(merged, full_out, preferred_element_type=jnp.float32)
    normed_two, inverse_two = rms_fwd(mixed, gain_two)
    h_second = normed_two.astype(jnp.bfloat16)
    pre_act = jnp.dot(h_second, full_up, preferred_element_type=jnp.float32) + up_bias
    act_low = jax.nn.silu(pre_act).astype(jnp.bfloat16)
    result = mixed + jnp.dot(act_low, full_down, preferred_element_type=jnp.float32) + down_bias
    cot_rows = out_cotangent[0]
    cot_float = cot_rows.astype(jnp.float32)
    grad_bdown = jnp.sum(cot_float, axis=0)
    grad_act = jnp.einsum("td,fd->tf", cot_rows, full_down, preferred_element_type=jnp.float32)
    sigmoid_pre = jax.nn.sigmoid(pre_act)
    grad_pre = (grad_act * sigmoid_pre * (1.0 + pre_act * (1.0 - sigmoid_pre))).astype(jnp.bfloat16)
    grad_bup = jnp.sum(grad_pre.astype(jnp.float32), axis=0)
    grad_h_second = jnp.einsum("tf,df->td", grad_pre, full_up, preferred_element_type=jnp.float32)
    grad_gain_two, grad_mixed_norm = rms_back(grad_h_second, mixed, inverse_two, gain_two)
    grad_mixed = cot_float + grad_mixed_norm
    branch_grad = grad_mixed.astype(jnp.bfloat16)
    grad_merged = jnp.einsum(
        "td,ed->te", branch_grad, full_out, preferred_element_type=jnp.float32
    ).astype(jnp.bfloat16)
    grad_rows = lax.all_to_all(grad_merged, "head", split_axis=1, concat_axis=0, tiled=True)
    grad_heads = split_heads(grad_rows, local_heads)
    deltas = jnp.einsum("rhd,hrd->hr", grad_heads.astype(jnp.float32), attention)
    whole_keys, whole_values, whole_ids = (
        lax.all_gather(key_rows, "blk", axis=0, tiled=True),
        lax.all_gather(value_rows, "blk", axis=0, tiled=True),
        lax.all_gather(query_ids, "blk", axis=0, tiled=True),
    )
    total_rows = whole_keys.shape[0]
    block_rows = block_rows_of(total_rows)
    block_count = total_rows // block_rows

    def key_step(grad_query_sum, block_piece):
        key_block, value_block, id_block = block_piece
        key_heads = split_heads(key_block, local_heads)
        value_heads = split_heads(value_block, local_heads)
        probs_low, grad_scores = probabilities(
            query_heads, grad_heads, log_sums, deltas, query_ids, key_heads, value_heads, id_block
        )
        grad_query_sum = grad_query_sum + jnp.einsum(
            "hrk,khd->hrd", grad_scores, key_heads, preferred_element_type=jnp.float32
        )
        key_term = jnp.einsum(
            "hrk,rhd->khd", grad_scores, query_heads, preferred_element_type=jnp.float32
        ).reshape(block_rows, -1)
        value_term = jnp.einsum(
            "hrk,rhd->khd", probs_low, grad_heads, preferred_element_type=jnp.float32
        ).reshape(block_rows, -1)
        return (grad_query_sum, jnp.stack((key_term, value_term), axis=1))

    grad_query_acc, key_terms = lax.scan(
        key_step,
        jnp.zeros((local_heads, row_count, HEAD_DIM), jnp.float32),
        (
            whole_keys.reshape(block_count, block_rows, -1),
            whole_values.reshape(block_count, block_rows, -1),
            whole_ids.reshape(block_count, block_rows),
        ),
    )
    summed = lax.psum_scatter(
        key_terms.reshape(total_rows, 2, -1).astype(jnp.bfloat16),
        "blk",
        scatter_dimension=0,
        tiled=True,
    ).astype(jnp.float32)
    grad_key_rows = summed[:, 0]
    grad_value_rows = summed[:, 1]
    grad_query_rows = (
        jnp.transpose(grad_query_acc, (1, 0, 2)).reshape(row_count, -1).astype(jnp.bfloat16)
    )
    back_query, back_key, back_value = (
        lax.all_to_all(grad_query_rows, "head", split_axis=0, concat_axis=1, tiled=True),
        lax.all_to_all(
            grad_key_rows.astype(jnp.bfloat16), "head", split_axis=0, concat_axis=1, tiled=True
        ),
        lax.all_to_all(
            grad_value_rows.astype(jnp.bfloat16), "head", split_axis=0, concat_axis=1, tiled=True
        ),
    )
    grad_q_scaled = back_query.astype(jnp.float32)
    scale_terms = jnp.sum(grad_q_scaled * q_raw, axis=0).reshape(HEADS, HEAD_DIM).sum(axis=0)
    scale_local = scale_terms * (scale_base / math.sqrt(HEAD_DIM)) * jax.nn.sigmoid(query_scale)
    grad_q_raw = (grad_q_scaled * factor).astype(jnp.bfloat16)
    grad_qkv_rows = jnp.concatenate([grad_q_raw, back_key, back_value], axis=1)
    grad_h_first = jnp.einsum(
        "te,de->td", grad_qkv_rows, full_qkv, preferred_element_type=jnp.float32
    )
    grad_gain_one, grad_x_norm = rms_back(grad_h_first, x_rows, inverse_one, gain_one)
    grad_x = grad_mixed + grad_x_norm
    term_qkv = jnp.einsum("tr,te->re", h_first, grad_qkv_rows, preferred_element_type=jnp.float32)
    term_out = jnp.einsum("tr,te->re", merged, branch_grad, preferred_element_type=jnp.float32)
    term_up = jnp.einsum("tr,te->re", h_second, grad_pre, preferred_element_type=jnp.float32)
    term_down = jnp.einsum("tr,te->re", act_low, cot_rows, preferred_element_type=jnp.float32)
    stacked = lax.psum_scatter(
        jnp.concatenate([term_qkv, term_out, term_up, term_down], axis=1),
        ("dp", "blk", "head"),
        scatter_dimension=0,
        tiled=True,
    )
    shares = (
        lax.psum_scatter(grad_gain_one, ("dp", "blk", "head"), scatter_dimension=0, tiled=True),
        lax.psum_scatter(grad_gain_two, ("dp", "blk", "head"), scatter_dimension=0, tiled=True),
        lax.psum_scatter(grad_bup, ("dp", "blk", "head"), scatter_dimension=0, tiled=True),
        lax.psum_scatter(grad_bdown, ("dp", "blk", "head"), scatter_dimension=0, tiled=True),
    )
    scale_total = lax.psum(scale_local, ("dp", "blk", "head"))
    share_qkv = stacked[:, : 3 * width]
    share_out = stacked[:, 3 * width : 4 * width]
    share_up = stacked[:, 4 * width : 5 * width]
    share_down = stacked[:, 5 * width :]
    return (
        result.astype(jnp.bfloat16)[None],
        grad_x[None],
        share_qkv,
        share_out,
        share_up,
        share_down,
        shares[0],
        shares[1],
        shares[2],
        shares[3],
        scale_total,
    )


BIT_X, BIT_C, BIT_Z1, BIT_Z0, BIT_Y = 16, 8, 4, 2, 1
AXES = ("dp", "blk", "head")
BF = jnp.bfloat16
F32 = jnp.float32


VMEM = pltpu.VMEM
NEG = -1e30


def call(body, outs, *args, vmem=16, scratch=(), smem=0, flops=0):
    spaces = [pltpu.SMEM if i < smem else VMEM for i in range(len(args))]
    return pl.pallas_call(
        body,
        out_shape=[jax.ShapeDtypeStruct(s, d) for s, d in outs],
        in_specs=[pl.BlockSpec(memory_space=s) for s in spaces],
        out_specs=[pl.BlockSpec(memory_space=VMEM) for _ in outs],
        scratch_shapes=list(scratch),
        compiler_params=pltpu.CompilerParams(vmem_limit_bytes=vmem << 20),
        cost_estimate=pl.CostEstimate(flops=int(flops), bytes_accessed=0, transcendentals=0),
    )(*args)


def mm(a, b, ca=1, cb=0):
    return lax.dot_general(a, b, (((ca,), (cb,)), ((), ())), preferred_element_type=F32)


def head_lanes(rows, width):
    return lax.broadcasted_iota(jnp.int32, (rows, width), 1) < HEAD_DIM


def attend_kernel(tok_ref, w_ref, factor_ref, o_ref, q_ref, k_ref, v_ref, raw_ref, lse_ref, vt_ref, row_ref):
    rows, hw = o_ref.shape
    width = w_ref.shape[0]
    step = 256
    for i in range(rows // step):
        at = slice(i * step, (i + 1) * step)
        qkv = mm(tok_ref[at, :width], w_ref[...])
        raw_ref[at, :] = qkv[:, :hw]
        q_ref[at, :] = (qkv[:, :hw] * factor_ref[0:1, :]).astype(BF)
        k_ref[at, :] = qkv[:, hw : 2 * hw].astype(BF)
        v = qkv[:, 2 * hw :]
        v_ref[at, :] = v.astype(BF)
        vt_ref[:, at] = v.T.astype(BF)
        row_ref[:, at] = tok_ref[at, width:].astype(F32).T[:8]
    id_col = tok_ref[:, width : width + 1].astype(F32)
    first = head_lanes(step, hw)

    def turn_body(i, carry):
        start = pl.multiple_of(i * step, step)
        at = pl.ds(start, step)
        q = q_ref[at, :]
        allowed = id_col <= row_ref[0:1, at]
        parts = []
        for h in range(2):
            q_head = jnp.where(first if h == 0 else jnp.logical_not(first), q, jnp.zeros_like(q))
            s = jnp.where(allowed, mm(k_ref[...], q_head, 1, 1), NEG)
            top = jnp.max(s, axis=0, keepdims=True)
            e = jnp.exp(s - top)
            total = jnp.sum(e, axis=0, keepdims=True)
            lse_ref[h : h + 1, at] = top + jnp.log(total)
            ot = mm(vt_ref[h * HEAD_DIM : (h + 1) * HEAD_DIM, :], e.astype(BF))
            parts.append(ot * (1.0 / total))
        o_ref[at, :] = jnp.concatenate(parts, axis=0).T.astype(BF)
        return carry

    lax.fori_loop(0, rows // step, turn_body, 0)


def attend(tokens, w, factor):
    rows, hw = tokens.shape[0], w.shape[1] // 3
    return call(
        attend_kernel,
        [((rows, hw), BF), ((rows, hw), BF), ((rows, hw), BF), ((rows, hw), BF), ((rows, hw), F32), ((8, rows), F32)],
        tokens, w, factor,
        scratch=[pltpu.VMEM((hw, rows), BF), pltpu.VMEM((8, rows), F32)],
        flops=2 * rows * (w.shape[0] * 3 * hw + 4 * rows * hw),
        vmem=24,
    )


def attend_back_kernel(tok_ref, factor_ref, do_ref, o_ref, q_ref, k_ref, v_ref, raw_ref, lse_ref,
                       d_ref, scale_ref, kt_ref, row_ref, dk_ref, dv_ref):
    rows, hw = o_ref.shape
    step = 256
    for i in range(rows // step):
        at = slice(i * step, (i + 1) * step)
        kt_ref[:, at] = k_ref[at, :].astype(F32).T.astype(BF)
        row_ref[:, at] = tok_ref[at, -128:].astype(F32).T[:8]
    id_col = tok_ref[:, -128:].astype(F32)[:, :1]
    first = head_lanes(step, hw)
    dk_ref[...] = jnp.zeros_like(dk_ref)
    dv_ref[...] = jnp.zeros_like(dv_ref)
    scale_ref[...] = jnp.zeros_like(scale_ref)

    def turn_body(i, carry):
        start = pl.multiple_of(i * step, step)
        at = pl.ds(start, step)
        q, d_o = q_ref[at, :], do_ref[at, :]
        allowed = id_col <= row_ref[0:1, at]
        prod = (d_o.astype(F32) * o_ref[at, :].astype(F32)).T
        parts = []
        for h in range(2):
            mine = first if h == 0 else jnp.logical_not(first)
            q_head = jnp.where(mine, q, jnp.zeros_like(q))
            do_head = jnp.where(mine, d_o, jnp.zeros_like(d_o))
            delta = jnp.sum(prod[h * HEAD_DIM : (h + 1) * HEAD_DIM], axis=0, keepdims=True)
            s = jnp.where(allowed, mm(k_ref[...], q_head, 1, 1), NEG)
            p = jnp.exp(s - lse_ref[h : h + 1, at])
            d_p = mm(v_ref[...], do_head, 1, 1)
            d_s = (p * (d_p - delta)).astype(BF)
            dv_ref[...] += mm(p.astype(BF), do_head)
            dk_ref[...] += mm(d_s, q_head)
            parts.append(mm(kt_ref[h * HEAD_DIM : (h + 1) * HEAD_DIM, :], d_s))
        d_q = jnp.concatenate(parts, axis=0).T.astype(BF).astype(F32)
        scale_ref[0:1, :] += jnp.sum(d_q * raw_ref[at, :], axis=0, keepdims=True)
        d_ref[at, :hw] = (d_q * factor_ref[0:1, :]).astype(BF)
        return carry

    lax.fori_loop(0, rows // step, turn_body, 0)
    d_ref[:, hw : 2 * hw] = dk_ref[...].astype(BF)
    d_ref[:, 2 * hw :] = dv_ref[...].astype(BF)


def attend_back(tokens, factor, d_o, o, q, k, v, raw, lse):
    rows, hw = o.shape
    return call(
        attend_back_kernel,
        [((rows, 3 * hw), BF), ((8, hw), F32)],
        tokens, factor, d_o, o, q, k, v, raw, lse,
        scratch=[pltpu.VMEM((hw, rows), BF), pltpu.VMEM((8, rows), F32), pltpu.VMEM((rows, hw), F32),
                 pltpu.VMEM((rows, hw), F32)],
        flops=2 * rows * 10 * rows * hw,
        vmem=24,
    )


def out_kernel(place_ref, p0, p1, p2, p3, wo_ref, own_ref, sib_ref):
    tok = own_ref.shape[0]
    hw = p0.shape[1]
    total = None
    for d, piece in enumerate((p0, p1, p2, p3)):
        at = pl.ds(pl.multiple_of(place_ref[d] * hw, 16), hw)
        term = mm(piece[...], wo_ref[at, :])
        total = term if total is None else total + term
    own_ref[...] = total[:tok]
    sib_ref[...] = total[tok:].astype(BF)


def norm_kernel(x_ref, own_ref, got_ref, x2_ref, n_ref):
    x2 = x_ref[...].astype(F32) + own_ref[...] + got_ref[...].astype(F32)
    x2_ref[...] = x2
    n_ref[...] = (x2 * lax.rsqrt(jnp.mean(x2 * x2, axis=-1, keepdims=True) + norm_eps)).astype(BF)


def pick_columns(rows, core, own):
    q = rows.shape[1] // 4
    odd = core if own else 1 - core
    parts = [jnp.where(odd == 1, rows[:, (2 * b + 1) * q : (2 * b + 2) * q], rows[:, 2 * b * q : (2 * b + 1) * q])
             for b in range(2)]
    return jnp.concatenate(parts, axis=1)


def mlp_kernel(place_ref, n_own_ref, n_sib_ref, cot_own_ref, cot_sib_ref, up_ref, dn_ref, extra_ref,
               act_ref, pre_ref, cols_ref, out_own_ref, out_sib_ref, d_own_ref, d_sib_ref):
    tok, width = n_own_ref.shape
    half = width // 2
    core = place_ref[4]
    n_pair = jnp.concatenate([n_own_ref[...], n_sib_ref[...]], axis=0).astype(F32)
    cols_ref[:, :half] = pick_columns(n_pair, core, True).astype(BF)
    cols_ref[:, half:] = pick_columns(n_pair, core, False).astype(BF)
    biases = extra_ref[...].astype(F32).T
    bias = biases[0:1]
    u = mm(cols_ref[:, :half], up_ref[:, :half]) + mm(cols_ref[:, half:], up_ref[:, half:]) + bias
    sig = jax.nn.sigmoid(u)
    act_ref[...] = (u * sig).astype(BF)
    slope = sig * (1.0 + u * (1.0 - sig))
    pre_ref[:tok] = (mm(cot_own_ref[...], dn_ref[...], 1, 1) * slope[:tok]).astype(BF)
    pre_ref[tok:] = (mm(cot_sib_ref[...], dn_ref[...], 1, 1) * slope[tok:]).astype(BF)
    d_own = mm(pre_ref[...], up_ref[:, :half], 1, 1)
    d_sib = mm(pre_ref[...], up_ref[:, half:], 1, 1)
    q = half // 2
    blocks = []
    for b in range(2):
        a, o = d_own[:, b * q : (b + 1) * q], d_sib[:, b * q : (b + 1) * q]
        blocks += [jnp.where(core == 1, o, a), jnp.where(core == 1, a, o)]
    d_n = jnp.concatenate(blocks, axis=1)
    d_own_ref[...] = d_n[:tok]
    d_sib_ref[...] = d_n[tok:].astype(BF)
    blocks = []
    for b in range(2):
        a = biases[1:2, b * q : (b + 1) * q]
        blocks += [jnp.where(core == 1, 0.0, a), jnp.where(core == 1, a, 0.0)]
    out = mm(act_ref[...], dn_ref[...]) + jnp.concatenate(blocks, axis=1)
    out_own_ref[...] = out[:tok]
    out_sib_ref[...] = out[tok:].astype(BF)


def norm_back_kernel(x2_ref, cot_ref, own_ref, got_ref, d_ref, low_ref):
    x2 = x2_ref[...]
    inverse = lax.rsqrt(jnp.mean(x2 * x2, axis=-1, keepdims=True) + norm_eps)
    normed = x2 * inverse
    d_n = own_ref[...] + got_ref[...].astype(F32)
    d_x = cot_ref[...].astype(F32) + inverse * (d_n - normed * jnp.mean(d_n * normed, axis=-1, keepdims=True))
    d_ref[...] = d_x
    low_ref[...] = d_x.astype(BF)


def attn_grad_kernel(place_ref, own_ref, sib_ref, wo_ref, g0, g1, g23):
    tok = own_ref.shape[0]
    hw = g0.shape[1]
    for d in range(4):
        at = pl.ds(pl.multiple_of(place_ref[d] * hw, 16), hw)
        w = wo_ref[at, :]
        for r, rows in enumerate((own_ref, sib_ref)):
            to = slice(r * tok, (r + 1) * tok)
            piece = mm(rows[...], w, 1, 1).astype(BF)
            if d < 2:
                (g0, g1)[d][to, :] = piece
            else:
                g23[d - 2, to, :] = piece


def mlp_grad_kernel(place_ref, cols_ref, pre_ref, act_ref, cot_own_ref, cot_sib_ref, g_up, g_dn):
    tok, width = cot_own_ref.shape
    half = width // 2
    core = place_ref[4]
    cot = jnp.concatenate([cot_own_ref[...], cot_sib_ref[...]], axis=0)
    act_t = act_ref[...].astype(F32).T.astype(BF)
    g_dn[:, :width] = mm(act_t, cot).astype(BF)
    for h in range(2):
        cols_t = cols_ref[:, h * half : (h + 1) * half].astype(F32).T.astype(BF)
        g_up[:, h * half : (h + 1) * half] = mm(cols_t, pre_ref[...]).astype(BF)
    s_up = jnp.sum(pre_ref[...].astype(F32), axis=0, keepdims=True)
    s_dn = pick_columns(jnp.sum(cot.astype(F32), axis=0, keepdims=True), core, True)
    rows = jnp.concatenate([s_up, s_dn, jnp.zeros((126, half), F32)], axis=0)
    g_dn[:, width:] = rows.T.astype(BF)


def out_grad_kernel(place_ref, p0, p1, p2, p3, own_ref, sib_ref, g_out):
    hw = p0.shape[1]
    d_branch = jnp.concatenate([own_ref[...], sib_ref[...]], axis=0)
    for d, piece in enumerate((p0, p1, p2, p3)):
        at = pl.ds(pl.multiple_of(place_ref[d] * hw, 16), hw)
        g_out[at, :] = mm(piece[...].astype(F32).T.astype(BF), d_branch).astype(BF)


def column(row):
    n = row.shape[1]
    same = lax.broadcasted_iota(jnp.int32, (n, n), 0) == lax.broadcasted_iota(jnp.int32, (n, n), 1)
    return jnp.sum(jnp.where(same, row, 0.0), axis=1, keepdims=True)


def row_of(col):
    n = col.shape[0]
    same = lax.broadcasted_iota(jnp.int32, (n, n), 0) == lax.broadcasted_iota(jnp.int32, (n, n), 1)
    return jnp.sum(jnp.where(same, col, 0.0), axis=0, keepdims=True)


def prep_kernel(place_ref, vec_ref, wq_ref, wo_ref, wu_ref, wd_ref, keep_ref, send_ref, up_keep_ref, up_send_ref, rest_ref):
    shard, width = wo_ref.shape
    hw = 2 * HEAD_DIM
    core = place_ref[4]
    wq = (wq_ref[...].astype(F32) * column(vec_ref[0:1, :])).astype(BF).astype(F32)
    for g in range(4):
        for t in range(3):
            base = t * width + (g // 2) * 4 * hw + (g % 2) * hw
            a, b = wq[:, base : base + hw], wq[:, base + 2 * hw : base + 3 * hw]
            to = slice(t * hw, (t + 1) * hw)
            keep_ref[place_ref[5 + g], :, to] = jnp.where(core == 1, b, a).astype(BF)
            send_ref[place_ref[9 + g], :, to] = jnp.where(core == 1, a, b).astype(BF)
    up = wu_ref[...].astype(F32) * column(vec_ref[1:2, :])
    up_keep_ref[...] = pick_columns(up, core, True).astype(BF)
    up_send_ref[...] = pick_columns(up, core, False).astype(BF)
    rest_ref[:, :width] = wo_ref[...]
    lane = lax.broadcasted_iota(jnp.int32, (shard, 128), 1)
    extra = jnp.where(lane == 0, column(vec_ref[2:3, :]), jnp.where(lane == 1, column(vec_ref[3:4, :]), 0.0))
    rest_ref[:, width : width + 128] = extra.astype(BF)
    rest_ref[:, width + 128 :] = wd_ref[...]


def first_norm_kernel(place_ref, x_ref, ids_ref, n_ref):
    tok, width = x_ref.shape
    x = x_ref[...].astype(F32)
    n_ref[:, :width] = (x * lax.rsqrt(jnp.mean(x * x, axis=-1, keepdims=True) + norm_eps)).astype(BF)
    ids = ids_ref[...].astype(F32)
    ids = jnp.where(place_ref[13] == 1, ids[:, tok:], ids[:, :tok])
    n_ref[:, width:] = jnp.broadcast_to(column(ids), (tok, 128)).astype(BF)


def token_grad_kernel(d_ref, w_ref, own_ref, sib_ref):
    tok = own_ref.shape[1]
    for i in range(4):
        d_n = mm(d_ref[2 * i * tok : 2 * (i + 1) * tok, :], w_ref[...], 1, 1)
        own_ref[i] = d_n[:tok].astype(BF)
        sib_ref[i] = d_n[tok:].astype(BF)


def pack_kernel(g_ref, scale_ref, factor_ref, out_ref):
    hw = 2 * HEAD_DIM
    terms = scale_ref[0:1, :HEAD_DIM] + scale_ref[0:1, HEAD_DIM:]
    terms = terms * factor_ref[1:2, :HEAD_DIM]
    terms = jnp.concatenate([terms, jnp.zeros((1, 16), F32)], axis=1)
    lines = jnp.concatenate([terms[:, 32 * i : 32 * (i + 1)] for i in range(3)] + [jnp.zeros((37, 32), F32)], axis=0)
    lines = jnp.concatenate([lines] * 4, axis=0).astype(BF)
    for r in range(8):
        x, c, z1 = r >> 2, (r >> 1) & 1, r & 1
        out_ref[2 * x + z1, c, :, : 3 * hw] = g_ref[r * hw : (r + 1) * hw, :]
        out_ref[2 * x + z1, c, :, 3 * hw :] = lines


def qkv_out_kernel(place_ref, vec_ref, g_ref, wq_ref, share_ref, gain_ref, scale_ref):
    shard = wq_ref.shape[0]
    width = wq_ref.shape[1] // 3
    hw = 2 * HEAD_DIM
    gain = column(vec_ref[0:1, :])
    total = jnp.zeros((shard, 1), F32)
    scale = jnp.zeros((8, 32), F32)
    for j in range(4):
        for c in range(2):
            piece = g_ref[place_ref[14 + j], c ^ place_ref[4]].astype(F32)
            scale = scale + piece[:8, 3 * hw :]
            for t in range(3):
                base = t * width + (j // 2) * 4 * hw + c * 2 * hw + (j % 2) * hw
                part = piece[:, t * hw : (t + 1) * hw]
                share_ref[:, base : base + hw] = part * gain
                total = total + jnp.sum(part * wq_ref[:, base : base + hw].astype(F32), axis=1, keepdims=True)
    gain_ref[...] = row_of(total)
    scale_ref[...] = scale


def rest_out_kernel(place_ref, vec_ref, a_ref, b_ref, wu_ref, out_ref, up_ref, dn_ref, gain_ref, bias_ref):
    width = out_ref.shape[1]
    half = width // 2
    q = half // 2
    core = place_ref[4]
    mine = a_ref[...].astype(F32) + b_ref[...].astype(F32)
    out_ref[...] = mine[:, :width]
    own, other = mine[:, width : width + half], mine[:, width + half : 2 * width]
    blocks = []
    for i in range(2):
        a, b = own[:, i * q : (i + 1) * q], other[:, i * q : (i + 1) * q]
        blocks += [jnp.where(core == 1, b, a), jnp.where(core == 1, a, b)]
    up = jnp.concatenate(blocks, axis=1)
    up_ref[...] = up * column(vec_ref[1:2, :])
    gain_ref[...] = row_of(jnp.sum(up * wu_ref[...].astype(F32), axis=1, keepdims=True))
    dn_ref[...] = mine[:, 2 * width : 3 * width]
    bias_ref[0:1, :] = row_of(mine[:, 3 * width : 3 * width + 1])
    bias_ref[1:2, :] = row_of(mine[:, 3 * width + 1 : 3 * width + 2])


def flip(array, mask_even, mask_odd):
    pairs = [(i, i ^ (mask_odd if i & BIT_C else mask_even)) for i in range(32)]
    return lax.ppermute(array, AXES, pairs)


def flip_core(array):
    return flip(array, BIT_C, BIT_C)


def turn(array):
    def other(i):
        c, z1 = (i // BIT_C) & 1, (i // BIT_Z1) & 1
        return (i & ~(BIT_C | BIT_Z1)) | (z1 * BIT_C) | (c * BIT_Z1)
    return lax.ppermute(array, AXES, [(i, other(i)) for i in range(32)])


def dot(a, b, dims):
    return lax.dot_general(a, b, (dims, ((), ())), preferred_element_type=F32)


def place(blocks, index_of, axis=0):
    out = jnp.zeros((len(blocks),) + blocks[0].shape, blocks[0].dtype)
    for d, block in enumerate(blocks):
        out = lax.dynamic_update_index_in_dim(out, block, index_of(d), 0)
    return out


def after(array, *others):
    return lax.optimization_barrier((array,) + others)[0]


def square_shards(block_input, block_ids, w_qkv, w_out, w_up, w_down, gain_attn, gain_mlp,
                  bias_up, bias_down, query_scale, out_cotangent):
    width = block_input.shape[2]
    tok = block_input.shape[1]
    shard = w_qkv.shape[0]
    half = width // 2
    hw = 2 * HEAD_DIM
    me = lax.axis_index(AXES)
    bit_x, bit_c, bit_z1, bit_z0, bit_y = [(me // b) & 1 for b in (16, 8, 4, 2, 1)]
    core = bit_c == 1
    j = me & 3
    first = jnp.where(core, BIT_Z0, BIT_Y)
    second = 3 - first
    disp = (0, first, second, 3)
    slot = lambda g, of_one: jnp.where((g ^ j) == 0, 0, jnp.where((g ^ j) == 3, 3, jnp.where((g ^ j) == 1, of_one, 3 - of_one)))
    places = jnp.stack(
        [j, j ^ first, j ^ second, j ^ 3, bit_c]
        + [slot(g, jnp.where(core, 1, 2)) for g in range(4)]
        + [slot(g, jnp.where(core, 2, 1)) for g in range(4)]
        + [bit_y]
        + [slot(g, jnp.where(core, 2, 1)) for g in range(4)]
    ).astype(jnp.int32)
    flip_first = lambda a: flip(a, BIT_Y, BIT_Z0)
    flip_second = lambda a: flip(a, BIT_Z0, BIT_Y)
    pick = lambda a, i, axis=0: lax.dynamic_index_in_dim(a, i, axis, keepdims=False)
    rows_f, rows_b = ((tok, width), F32), ((tok, width), BF)

    x_low = turn(block_input[0])
    ids_low = turn(block_ids)

    vectors = jnp.stack([gain_attn, gain_mlp, bias_up, bias_down]).astype(F32)
    keep, send, up_keep, up_send, rest = call(
        prep_kernel,
        [((4, shard, 3 * hw), BF), ((4, shard, 3 * hw), BF), ((shard, half), BF), ((shard, half), BF),
         ((shard, 2 * width + 128), BF)],
        places, vectors, w_qkv, w_out, w_up, w_down, smem=1)
    sib = flip_core(send)
    up_sib = flip_core(up_send)

    got = flip_first(jnp.stack([keep[2:], sib[2:]]))
    pay = jnp.concatenate([rest, up_keep, up_sib], axis=1)
    pay = place([pay, flip(after(pay, sib), BIT_Z1, BIT_Z1)], lambda d: bit_z1 ^ d)
    got2 = flip_second(jnp.stack([keep[1], sib[1], got[0, 1], got[1, 1]]))
    sources = [(keep[0], sib[0]), (got[0, 0], got[1, 0]), (got2[0], got2[1]), (got2[2], got2[3])]
    grid = jnp.zeros((2, 4, shard, 3 * hw), BF)
    for d, pair in enumerate(sources):
        for o, block in enumerate(pair):
            grid = lax.dynamic_update_slice(grid, block[None, None], (bit_c ^ o, j ^ disp[d], 0, 0))
    grid = grid.reshape(2, 4 * shard, 3 * hw)
    a1 = flip(grid, BIT_X, BIT_Z1)
    a2 = flip(jnp.stack([grid, a1]), BIT_Z1, BIT_X)
    k_now = bit_x * 2 + bit_z1
    d_first = jnp.where(core, 1, 2)
    wq_full = place([grid, a1, a2[0], a2[1]], lambda d: k_now ^ (0, d_first, 3 - d_first, 3)[d])
    wq_full = wq_full.reshape(2, 2, 2, 4 * shard, 3 * hw).transpose(0, 2, 1, 3, 4).reshape(width, 3 * hw)

    (n_msg,) = call(first_norm_kernel, [((tok, width + 128), BF)], places, x_low, ids_low, smem=1)
    r1 = flip_first(n_msg)
    r2 = flip_second(jnp.concatenate([n_msg, r1], axis=0))
    m0, m1, m2 = flip_core(n_msg), flip_core(r1), flip_core(r2)
    tokens = jnp.concatenate(
        [n_msg, m0, r1, m2[:tok], r2[:tok], m1, r2[tok:], m2[tok:]], axis=0)

    bits = {"x": (BIT_X, bit_x, 0), "z": (BIT_Z0, bit_z0, 2), "y": (BIT_Y, bit_y, 3)}

    def spread(block, order, gates):
        block = block[None, :, None, None]
        for name, gate in zip(order, gates, strict=True):
            mask, bit, axis = bits[name]
            other = flip(after(block, gate), mask, mask)
            block = jnp.concatenate([jnp.where(bit == 1, other, block), jnp.where(bit == 1, block, other)], axis=axis)
        return block.reshape(half, -1)

    cut = width + 128
    gates = (r1, a1, r2)
    wo_all = spread(pay[..., :cut], "zyx", gates)
    dn_all = spread(pay[..., cut : cut + width], "xzy", gates)
    up_all = spread(pay[..., cut + width :], "yxz", gates)
    wo, extra_all = wo_all[:, :width], wo_all[:, width:]
    cot_own = turn(after(out_cotangent[0], a1))
    cot_sib = flip_core(cot_own)

    base = scale_base / math.sqrt(HEAD_DIM)
    factor = jnp.stack([jnp.tile(base * jax.nn.softplus(query_scale), 2), jnp.tile(base * jax.nn.sigmoid(query_scale), 2)])
    attn_out, q_h, k_h, v_h, q_raw, lse = attend(tokens, wq_full, factor)
    attn = attn_out.reshape(4, 2 * tok, hw)
    s1 = flip_first(jnp.stack([attn[1], attn[3]]))
    s2 = flip_second(jnp.stack([attn[2], s1[1]]))
    heads = (attn[0], s1[0], s2[0], s2[1])

    part, part_sib = call(out_kernel, [rows_f, rows_b], places, *heads, wo, smem=1)
    x2, n_two = call(norm_kernel, [rows_f, rows_b], x_low, part, flip_core(part_sib), vmem=8)
    act, d_pre, n_cols, out_own, out_sib, d_own, d_sib = call(
        mlp_kernel,
        [((2 * tok, half), BF), ((2 * tok, half), BF), ((2 * tok, width), BF), rows_f, rows_b, rows_f, rows_b],
        places, n_two, flip_core(n_two), cot_own, cot_sib, up_all, dn_all, extra_all, smem=1, vmem=24)
    d_x2, d_branch = call(norm_back_kernel, [rows_f, rows_b], x2, cot_own, d_own, flip_core(d_sib), vmem=8)
    branch_sib = flip_core(d_branch)
    g_up, g_dn = call(
        mlp_grad_kernel, [((half, width), BF), ((half, cut), BF)],
        places, n_cols, d_pre, act, cot_own, cot_sib, smem=1, vmem=24)
    da0, da1, da23 = call(
        attn_grad_kernel, [((2 * tok, hw), BF), ((2 * tok, hw), BF), ((2, 2 * tok, hw), BF)],
        places, d_branch, branch_sib, wo, smem=1)
    (g_out,) = call(out_grad_kernel, [((half, width), BF)], places, *heads, d_branch, branch_sib, smem=1)

    e = flip_second(da23)
    t = flip_first(jnp.stack([da1, e[1]]))
    d_o = jnp.concatenate([da0, t[0], e[0], t[1]], axis=0)
    d_qkv, scale_row = attend_back(tokens, factor, d_o, attn_out, q_h, k_h, v_h, q_raw, lse)

    out = x2 + out_own + flip_core(after(out_sib, t)).astype(F32)
    out = turn(out.astype(BF))

    def collect(grads, order, gate=None):
        grads = grads.reshape(2, 2, 2, 2, shard, -1)
        for name in order:
            mask, bit, axis = bits[name]
            other = pick(grads, 1 - bit, axis)
            if gate is not None:
                other, gate = after(other, gate), None
            other = flip(other, mask, mask)
            grads = (pick(grads, bit, axis).astype(F32) + other.astype(F32)).astype(BF)
            grads = jnp.expand_dims(grads, axis)
        return grads.reshape(2, shard, -1)

    c_dn = collect(g_dn, "xyz")
    c_up = collect(g_up, "yzx", t)
    c_out = collect(g_out, "zxy", t)
    c_up = jnp.concatenate([c_up[..., :half], flip_core(c_up[..., half:])], axis=2)
    c_all = jnp.concatenate([c_out, c_up, c_dn], axis=2)
    share_out, share_up, share_down, grad_gain_two, grad_bias = call(
        rest_out_kernel,
        [((shard, width), F32), ((shard, width), F32), ((shard, width), F32), ((1, shard), F32), ((2, shard), F32)],
        places, vectors, pick(c_all, bit_z1), flip(pick(c_all, 1 - bit_z1), BIT_Z1, BIT_Z1), w_up, smem=1)

    g_qkv = mm(tokens[:, :width], d_qkv, 0, 0).astype(BF)
    (g_qkv,) = call(pack_kernel, [((4, 2, 4 * shard, 512), BF)], g_qkv, scale_row, factor)
    qd = jnp.where(core, 2, 1)
    v1 = flip(jnp.stack([pick(g_qkv, k_now ^ qd), pick(g_qkv, k_now ^ 3)]), BIT_Z1, BIT_X).astype(F32)
    v2 = flip((pick(g_qkv, k_now ^ (3 - qd)).astype(F32) + v1[1]).astype(BF), BIT_X, BIT_Z1).astype(F32)
    gq = (pick(g_qkv, k_now).astype(F32) + v1[0] + v2).astype(BF)
    gq = gq.reshape(2, 4, shard, 512)
    pairs = jnp.stack([pick(gq, bit_c), flip_core(pick(gq, 1 - bit_c))], axis=1)
    rel = [pick(pairs, j ^ d) for d in disp]
    got = flip_first(jnp.stack([rel[1], rel[3]]))
    got2 = flip_second(jnp.stack([rel[2], got[1]]))
    share_qkv, grad_gain_one, scale = call(
        qkv_out_kernel, [((shard, 3 * width), F32), ((1, shard), F32), ((8, 32), F32)],
        places, vectors, jnp.stack([rel[0], got[0], got2[0], got2[1]]), w_qkv, smem=1)
    scale_total = scale[:3].reshape(96)[:HEAD_DIM]

    d_n, d_n_sib = call(
        token_grad_kernel, [((4, tok, width), BF), ((4, tok, width), BF)], after(d_qkv, g_qkv), wq_full)
    d_n = d_n.astype(F32)
    from_sib = flip_core(d_n_sib).astype(F32)
    td = [d_n[0] + from_sib[0], d_n[1] + from_sib[2], d_n[2] + from_sib[1], d_n[3] + from_sib[3]]
    p1 = flip_second(jnp.stack([td[2], td[3]]).astype(BF)).astype(F32)
    p2 = flip_first((td[1] + p1[1]).astype(BF)).astype(F32)
    d_n_one = td[0] + p1[0] + p2
    x_rows = x_low.astype(F32)
    inv_one = lax.rsqrt(jnp.mean(x_rows * x_rows, axis=-1, keepdims=True) + norm_eps)
    norm_one = x_rows * inv_one
    mean_one = jnp.mean(d_n_one * norm_one, axis=-1, keepdims=True)
    grad_x = d_x2 + inv_one * (d_n_one - norm_one * mean_one)
    grad_x = turn(grad_x.astype(BF)).astype(F32)
    return (out[None], grad_x[None], share_qkv, share_out, share_up, share_down,
            grad_gain_one.reshape(shard), grad_gain_two.reshape(shard), grad_bias[0], grad_bias[1], scale_total)


def solution(mesh):
    placed = (
        P("dp", ("blk", "head"), None),
        P("dp", "blk"),
        P(("dp", "blk", "head"), None),
        P(("dp", "blk", "head"), None),
        P(("dp", "blk", "head"), None),
        P(("dp", "blk", "head"), None),
        P(("dp", "blk", "head")),
        P(("dp", "blk", "head")),
        P(("dp", "blk", "head")),
        P(("dp", "blk", "head")),
        P(),
        P("dp", ("blk", "head"), None),
    )
    square = dict(mesh.shape) == {"dp": 4, "blk": 4, "head": 2}
    return jax.shard_map(
        square_shards if square else shards,
        mesh=mesh,
        in_specs=placed,
        out_specs=(
            P("dp", ("blk", "head"), None),
            P("dp", ("blk", "head"), None),
            P(("dp", "blk", "head"), None),
            P(("dp", "blk", "head"), None),
            P(("dp", "blk", "head"), None),
            P(("dp", "blk", "head"), None),
            P(("dp", "blk", "head")),
            P(("dp", "blk", "head")),
            P(("dp", "blk", "head")),
            P(("dp", "blk", "head")),
            P(),
        ),
        check_vma=False,
    )
```

```python
from functools import partial
import math

import jax
import jax.numpy as jnp
from jax import lax
from jax.experimental import pallas as pl
from jax.experimental.pallas import tpu as pltpu
from jax.sharding import Mesh, PartitionSpec as P

HEADS = 16
HEAD_DIM = 80


norm_eps = 1e-06
scale_base = 1.442695041


def rms_fwd(values_in, gain):
    inverse = lax.rsqrt(jnp.mean(values_in * values_in, axis=-1, keepdims=True) + norm_eps)
    return (values_in * inverse * gain, inverse)


def rms_back(incoming, values_in, inverse, gain):
    normed = values_in * inverse
    gain_grad = jnp.sum(incoming * normed, axis=0)
    scaled = incoming * gain
    input_grad = inverse * (scaled - normed * jnp.mean(scaled * normed, axis=-1, keepdims=True))
    return (gain_grad, input_grad)


def block_rows_of(row_count):
    return math.gcd(row_count, 512)


def sweep_rows(step_fn, running, pieces):
    row_count = pieces[0].shape[0]
    block_rows = block_rows_of(row_count)
    block_count = row_count // block_rows

    def turn_body(turn_index, current):
        sub_piece = tuple(
            (
                lax.dynamic_slice_in_dim(array_in, turn_index * block_rows, block_rows, 0)
                for array_in in pieces
            )
        )
        return step_fn(current, sub_piece)

    return lax.fori_loop(0, block_count, turn_body, running)


def split_heads(rows_in, head_count):
    return rows_in.reshape(rows_in.shape[0], head_count, -1)


def attend_step(query_heads, query_ids, running, sub_piece):
    maxima, totals, weighted = running
    key_rows, value_rows, key_ids = sub_piece
    key_heads = split_heads(key_rows, query_heads.shape[1])
    value_heads = split_heads(value_rows, query_heads.shape[1])
    scores = jnp.einsum("rhd,khd->hrk", query_heads, key_heads, preferred_element_type=jnp.float32)
    allowed = (key_ids[None, :] <= query_ids[:, None])[None]
    scores = jnp.where(allowed, scores, -1e30)
    new_max = jnp.maximum(maxima, jnp.max(scores, axis=-1))
    rescale = jnp.exp(maxima - new_max)
    weights = jnp.where(allowed, jnp.exp(scores - new_max[..., None]), 0.0)
    totals = totals * rescale + jnp.sum(weights, axis=-1)
    weighted = weighted * rescale[..., None] + jnp.einsum(
        "hrk,khd->hrd",
        weights.astype(jnp.bfloat16),
        value_heads,
        preferred_element_type=jnp.float32,
    )
    return (new_max, totals, weighted)


def probabilities(
    query_heads, grad_heads, log_sums, deltas, query_ids, key_heads, value_heads, key_ids
):
    scores = jnp.einsum("rhd,khd->hrk", query_heads, key_heads, preferred_element_type=jnp.float32)
    allowed = (key_ids[None, :] <= query_ids[:, None])[None]
    scores = jnp.where(allowed, scores, -1e30)
    probs = jnp.where(allowed, jnp.exp(scores - log_sums[..., None]), 0.0)
    grad_probs = jnp.einsum(
        "rhd,khd->hrk", grad_heads, value_heads, preferred_element_type=jnp.float32
    )
    grad_scores = probs * (grad_probs - deltas[..., None])
    return (probs.astype(jnp.bfloat16), grad_scores.astype(jnp.bfloat16))


def shards(
    block_input,
    block_ids,
    w_qkv,
    w_out,
    w_up,
    w_down,
    gain_attn,
    gain_mlp,
    bias_up,
    bias_down,
    query_scale,
    out_cotangent,
):
    gathered = (
        lax.all_gather(w_qkv, ("dp", "blk", "head"), axis=0, tiled=True),
        lax.all_gather(w_out, ("dp", "blk", "head"), axis=0, tiled=True),
        lax.all_gather(w_up, ("dp", "blk", "head"), axis=0, tiled=True),
        lax.all_gather(w_down, ("dp", "blk", "head"), axis=0, tiled=True),
        lax.all_gather(gain_attn, ("dp", "blk", "head"), axis=0, tiled=True),
        lax.all_gather(gain_mlp, ("dp", "blk", "head"), axis=0, tiled=True),
        lax.all_gather(bias_up, ("dp", "blk", "head"), axis=0, tiled=True),
        lax.all_gather(bias_down, ("dp", "blk", "head"), axis=0, tiled=True),
    )
    full_qkv, full_out, full_up, full_down = (gathered[0], gathered[1], gathered[2], gathered[3])
    gain_one = gathered[4].astype(jnp.float32)
    gain_two = gathered[5].astype(jnp.float32)
    up_bias = gathered[6].astype(jnp.float32)
    down_bias = gathered[7].astype(jnp.float32)
    width = block_input.shape[2]
    local_heads = HEADS // lax.axis_size("head")
    x_rows = block_input[0].astype(jnp.float32)
    query_ids = block_ids[0]
    normed_one, inverse_one = rms_fwd(x_rows, gain_one)
    h_first = normed_one.astype(jnp.bfloat16)
    qkv = jnp.dot(h_first, full_qkv, preferred_element_type=jnp.float32)
    q_raw = qkv[:, :width]
    factor = jnp.tile(scale_base / math.sqrt(HEAD_DIM) * jax.nn.softplus(query_scale), HEADS)
    q_scaled = (q_raw * factor).astype(jnp.bfloat16)
    key_low = qkv[:, width : 2 * width].astype(jnp.bfloat16)
    value_low = qkv[:, 2 * width :].astype(jnp.bfloat16)
    query_rows, key_rows, value_rows = (
        lax.all_to_all(q_scaled, "head", split_axis=1, concat_axis=0, tiled=True),
        lax.all_to_all(key_low, "head", split_axis=1, concat_axis=0, tiled=True),
        lax.all_to_all(value_low, "head", split_axis=1, concat_axis=0, tiled=True),
    )
    row_count = query_rows.shape[0]
    query_heads = split_heads(query_rows, local_heads)
    start_state = (
        jnp.full((local_heads, row_count), -1e30, jnp.float32),
        jnp.zeros((local_heads, row_count), jnp.float32),
        jnp.zeros((local_heads, row_count, HEAD_DIM), jnp.float32),
    )
    maxima, totals, weighted = sweep_rows(
        partial(attend_step, query_heads, query_ids),
        start_state,
        (
            lax.all_gather(key_rows, "blk", axis=0, tiled=True),
            lax.all_gather(value_rows, "blk", axis=0, tiled=True),
            lax.all_gather(query_ids, "blk", axis=0, tiled=True),
        ),
    )
    log_sums = maxima + jnp.log(totals)
    attention = weighted / totals[..., None]
    attn_rows = jnp.transpose(attention, (1, 0, 2)).reshape(row_count, -1).astype(jnp.bfloat16)
    merged = lax.all_to_all(attn_rows, "head", split_axis=0, concat_axis=1, tiled=True)
    mixed = x_rows + jnp.dot(merged, full_out, preferred_element_type=jnp.float32)
    normed_two, inverse_two = rms_fwd(mixed, gain_two)
    h_second = normed_two.astype(jnp.bfloat16)
    pre_act = jnp.dot(h_second, full_up, preferred_element_type=jnp.float32) + up_bias
    act_low = jax.nn.silu(pre_act).astype(jnp.bfloat16)
    result = mixed + jnp.dot(act_low, full_down, preferred_element_type=jnp.float32) + down_bias
    cot_rows = out_cotangent[0]
    cot_float = cot_rows.astype(jnp.float32)
    grad_bdown = jnp.sum(cot_float, axis=0)
    grad_act = jnp.einsum("td,fd->tf", cot_rows, full_down, preferred_element_type=jnp.float32)
    sigmoid_pre = jax.nn.sigmoid(pre_act)
    grad_pre = (grad_act * sigmoid_pre * (1.0 + pre_act * (1.0 - sigmoid_pre))).astype(jnp.bfloat16)
    grad_bup = jnp.sum(grad_pre.astype(jnp.float32), axis=0)
    grad_h_second = jnp.einsum("tf,df->td", grad_pre, full_up, preferred_element_type=jnp.float32)
    grad_gain_two, grad_mixed_norm = rms_back(grad_h_second, mixed, inverse_two, gain_two)
    grad_mixed = cot_float + grad_mixed_norm
    branch_grad = grad_mixed.astype(jnp.bfloat16)
    grad_merged = jnp.einsum(
        "td,ed->te", branch_grad, full_out, preferred_element_type=jnp.float32
    ).astype(jnp.bfloat16)
    grad_rows = lax.all_to_all(grad_merged, "head", split_axis=1, concat_axis=0, tiled=True)
    grad_heads = split_heads(grad_rows, local_heads)
    deltas = jnp.einsum("rhd,hrd->hr", grad_heads.astype(jnp.float32), attention)
    whole_keys, whole_values, whole_ids = (
        lax.all_gather(key_rows, "blk", axis=0, tiled=True),
        lax.all_gather(value_rows, "blk", axis=0, tiled=True),
        lax.all_gather(query_ids, "blk", axis=0, tiled=True),
    )
    total_rows = whole_keys.shape[0]
    block_rows = block_rows_of(total_rows)
    block_count = total_rows // block_rows

    def key_step(grad_query_sum, block_piece):
        key_block, value_block, id_block = block_piece
        key_heads = split_heads(key_block, local_heads)
        value_heads = split_heads(value_block, local_heads)
        probs_low, grad_scores = probabilities(
            query_heads, grad_heads, log_sums, deltas, query_ids, key_heads, value_heads, id_block
        )
        grad_query_sum = grad_query_sum + jnp.einsum(
            "hrk,khd->hrd", grad_scores, key_heads, preferred_element_type=jnp.float32
        )
        key_term = jnp.einsum(
            "hrk,rhd->khd", grad_scores, query_heads, preferred_element_type=jnp.float32
        ).reshape(block_rows, -1)
        value_term = jnp.einsum(
            "hrk,rhd->khd", probs_low, grad_heads, preferred_element_type=jnp.float32
        ).reshape(block_rows, -1)
        return (grad_query_sum, jnp.stack((key_term, value_term), axis=1))

    grad_query_acc, key_terms = lax.scan(
        key_step,
        jnp.zeros((local_heads, row_count, HEAD_DIM), jnp.float32),
        (
            whole_keys.reshape(block_count, block_rows, -1),
            whole_values.reshape(block_count, block_rows, -1),
            whole_ids.reshape(block_count, block_rows),
        ),
    )
    summed = lax.psum_scatter(
        key_terms.reshape(total_rows, 2, -1).astype(jnp.bfloat16),
        "blk",
        scatter_dimension=0,
        tiled=True,
    ).astype(jnp.float32)
    grad_key_rows = summed[:, 0]
    grad_value_rows = summed[:, 1]
    grad_query_rows = (
        jnp.transpose(grad_query_acc, (1, 0, 2)).reshape(row_count, -1).astype(jnp.bfloat16)
    )
    back_query, back_key, back_value = (
        lax.all_to_all(grad_query_rows, "head", split_axis=0, concat_axis=1, tiled=True),
        lax.all_to_all(
            grad_key_rows.astype(jnp.bfloat16), "head", split_axis=0, concat_axis=1, tiled=True
        ),
        lax.all_to_all(
            grad_value_rows.astype(jnp.bfloat16), "head", split_axis=0, concat_axis=1, tiled=True
        ),
    )
    grad_q_scaled = back_query.astype(jnp.float32)
    scale_terms = jnp.sum(grad_q_scaled * q_raw, axis=0).reshape(HEADS, HEAD_DIM).sum(axis=0)
    scale_local = scale_terms * (scale_base / math.sqrt(HEAD_DIM)) * jax.nn.sigmoid(query_scale)
    grad_q_raw = (grad_q_scaled * factor).astype(jnp.bfloat16)
    grad_qkv_rows = jnp.concatenate([grad_q_raw, back_key, back_value], axis=1)
    grad_h_first = jnp.einsum(
        "te,de->td", grad_qkv_rows, full_qkv, preferred_element_type=jnp.float32
    )
    grad_gain_one, grad_x_norm = rms_back(grad_h_first, x_rows, inverse_one, gain_one)
    grad_x = grad_mixed + grad_x_norm
    term_qkv = jnp.einsum("tr,te->re", h_first, grad_qkv_rows, preferred_element_type=jnp.float32)
    term_out = jnp.einsum("tr,te->re", merged, branch_grad, preferred_element_type=jnp.float32)
    term_up = jnp.einsum("tr,te->re", h_second, grad_pre, preferred_element_type=jnp.float32)
    term_down = jnp.einsum("tr,te->re", act_low, cot_rows, preferred_element_type=jnp.float32)
    stacked = lax.psum_scatter(
        jnp.concatenate([term_qkv, term_out, term_up, term_down], axis=1),
        ("dp", "blk", "head"),
        scatter_dimension=0,
        tiled=True,
    )
    shares = (
        lax.psum_scatter(grad_gain_one, ("dp", "blk", "head"), scatter_dimension=0, tiled=True),
        lax.psum_scatter(grad_gain_two, ("dp", "blk", "head"), scatter_dimension=0, tiled=True),
        lax.psum_scatter(grad_bup, ("dp", "blk", "head"), scatter_dimension=0, tiled=True),
        lax.psum_scatter(grad_bdown, ("dp", "blk", "head"), scatter_dimension=0, tiled=True),
    )
    scale_total = lax.psum(scale_local, ("dp", "blk", "head"))
    share_qkv = stacked[:, : 3 * width]
    share_out = stacked[:, 3 * width : 4 * width]
    share_up = stacked[:, 4 * width : 5 * width]
    share_down = stacked[:, 5 * width :]
    return (
        result.astype(jnp.bfloat16)[None],
        grad_x[None],
        share_qkv,
        share_out,
        share_up,
        share_down,
        shares[0],
        shares[1],
        shares[2],
        shares[3],
        scale_total,
    )


BIT_X, BIT_C, BIT_Z1, BIT_Z0, BIT_Y = 16, 8, 4, 2, 1
AXES = ("x", "c", "z1", "z0", "y")
BF = jnp.bfloat16
F32 = jnp.float32


VMEM = pltpu.VMEM
NEG = -1e30


def call(body, outs, *args, vmem=16, scratch=(), smem=0, hbm=()):
    spaces = [pltpu.SMEM if i < smem else pl.ANY if i in hbm else VMEM for i in range(len(args))]
    return pl.pallas_call(
        body,
        out_shape=[jax.ShapeDtypeStruct(s, d) for s, d in outs],
        in_specs=[pl.BlockSpec(memory_space=s) for s in spaces],
        out_specs=[pl.BlockSpec(memory_space=VMEM) for _ in outs],
        scratch_shapes=list(scratch),
        compiler_params=pltpu.CompilerParams(vmem_limit_bytes=vmem << 20),
        cost_estimate=pl.CostEstimate(flops=0, bytes_accessed=0, transcendentals=0),
    )(*args)


def mm(a, b, ca=1, cb=0):
    return lax.dot_general(a, b, (((ca,), (cb,)), ((), ())), preferred_element_type=F32)


def head_lanes(rows, width):
    return lax.broadcasted_iota(jnp.int32, (rows, width), 1) < HEAD_DIM


def attend_kernel(tok_ref, w_ref, factor_ref, o_ref, q_ref, k_ref, v_ref, raw_ref, lse_ref, vt_ref, row_ref):
    rows, hw = q_ref.shape
    width = w_ref.shape[0]
    step = 256
    for i in range(rows // step):
        at = slice(i * step, (i + 1) * step)
        qkv = mm(tok_ref[at, :width], w_ref[...])
        raw_ref[at, :] = qkv[:, :hw]
        q_ref[at, :] = (qkv[:, :hw] * factor_ref[0:1, :]).astype(BF)
        k_ref[at, :] = qkv[:, hw : 2 * hw].astype(BF)
        v = qkv[:, 2 * hw :]
        v_ref[at, :] = v.astype(BF)
        vt_ref[:, at] = v.T.astype(BF)
        row_ref[:, at] = tok_ref[at, width:].astype(F32).T[:8]
    id_col = tok_ref[:, width : width + 1].astype(F32)
    first = head_lanes(step, hw)

    def turn_body(i, carry):
        start = pl.multiple_of(i * step, step)
        at = pl.ds(start, step)
        q = q_ref[at, :]
        allowed = id_col <= row_ref[0:1, at]
        parts = []
        for h in range(2):
            q_head = jnp.where(first if h == 0 else jnp.logical_not(first), q, jnp.zeros_like(q))
            s = jnp.where(allowed, mm(k_ref[...], q_head, 1, 1), NEG)
            top = jnp.max(s, axis=0, keepdims=True)
            e = jnp.exp(s - top)
            total = jnp.sum(e, axis=0, keepdims=True)
            lse_ref[h : h + 1, at] = top + jnp.log(total)
            ot = mm(vt_ref[h * HEAD_DIM : (h + 1) * HEAD_DIM, :], e.astype(BF))
            parts.append(ot * (1.0 / total))
        o_ref[i] = jnp.concatenate(parts, axis=0).T.astype(BF)
        return carry

    lax.fori_loop(0, rows // step, turn_body, 0)


def attend(tokens, w, factor):
    rows, hw = tokens.shape[0], w.shape[1] // 3
    return call(
        attend_kernel,
        [((4, rows // 4, hw), BF), ((rows, hw), BF), ((rows, hw), BF), ((rows, hw), BF), ((rows, hw), F32), ((8, rows), F32)],
        tokens, w, factor,
        scratch=[pltpu.VMEM((hw, rows), BF), pltpu.VMEM((8, rows), F32)],
        vmem=24,
    )


def attend_back_kernel(place_ref, tok_ref, factor_ref, do_ref, o_ref, q_ref, k_ref, v_ref, raw_ref, lse_ref,
                       d_ref, keep_ref, send_ref, kt_ref, row_ref, dk_ref, dv_ref, scale_ref, grad_ref):
    rows, hw = q_ref.shape
    step = 256
    for i in range(rows // step):
        at = slice(i * step, (i + 1) * step)
        kt_ref[:, at] = k_ref[at, :].astype(F32).T.astype(BF)
        row_ref[:, at] = tok_ref[at, -128:].astype(F32).T[:8]
    id_col = tok_ref[:, -128:].astype(F32)[:, :1]
    first = head_lanes(step, hw)
    dk_ref[...] = jnp.zeros_like(dk_ref)
    dv_ref[...] = jnp.zeros_like(dv_ref)
    scale_ref[...] = jnp.zeros_like(scale_ref)

    def turn_body(i, carry):
        start = pl.multiple_of(i * step, step)
        at = pl.ds(start, step)
        q, d_o = q_ref[at, :], do_ref[at, :]
        allowed = id_col <= row_ref[0:1, at]
        prod = (d_o.astype(F32) * o_ref[i].astype(F32)).T
        parts = []
        for h in range(2):
            mine = first if h == 0 else jnp.logical_not(first)
            q_head = jnp.where(mine, q, jnp.zeros_like(q))
            do_head = jnp.where(mine, d_o, jnp.zeros_like(d_o))
            delta = jnp.sum(prod[h * HEAD_DIM : (h + 1) * HEAD_DIM], axis=0, keepdims=True)
            s = jnp.where(allowed, mm(k_ref[...], q_head, 1, 1), NEG)
            p = jnp.exp(s - lse_ref[h : h + 1, at])
            d_p = mm(v_ref[...], do_head, 1, 1)
            d_s = (p * (d_p - delta)).astype(BF)
            dv_ref[...] += mm(p.astype(BF), do_head)
            dk_ref[...] += mm(d_s, q_head)
            parts.append(mm(kt_ref[h * HEAD_DIM : (h + 1) * HEAD_DIM, :], d_s))
        d_q = jnp.concatenate(parts, axis=0).T.astype(BF).astype(F32)
        scale_ref[0:1, :] += jnp.sum(d_q * raw_ref[at, :], axis=0, keepdims=True)
        d_ref[at, :hw] = (d_q * factor_ref[0:1, :]).astype(BF)
        return carry

    lax.fori_loop(0, rows // step, turn_body, 0)
    d_ref[:, hw : 2 * hw] = dk_ref[...].astype(BF)
    d_ref[:, 2 * hw :] = dv_ref[...].astype(BF)

    width = grad_ref.shape[0]
    for i in range(width // 128):
        at = slice(i * 128, (i + 1) * 128)
        grad_ref[at, :] = mm(tok_ref[:, at], d_ref[...], 0, 0)
    terms = scale_ref[0:1, :HEAD_DIM] + scale_ref[0:1, HEAD_DIM:]
    terms = jnp.concatenate([terms * factor_ref[1:2, :HEAD_DIM], jnp.zeros((1, 16), F32)], axis=1)
    lines = jnp.concatenate([terms[:, 32 * i : 32 * (i + 1)] for i in range(3)] + [jnp.zeros((37, 32), F32)], axis=0)
    lines = jnp.concatenate([lines] * 4, axis=0).astype(BF)
    core = place_ref[4]
    for far, out in enumerate((keep_ref, send_ref)):
        for near in range(2):
            x = place_ref[2] ^ jnp.where(core == 1, far, near)
            z1 = place_ref[5] ^ jnp.where(core == 1, near, far)
            for c in range(2):
                at = pl.ds(pl.multiple_of((x * 4 + c * 2 + z1) * hw, 16), hw)
                out[near, c, :, : 3 * hw] = grad_ref[at, :].astype(BF)
                out[near, c, :, 3 * hw :] = lines


def attend_back(places, tokens, factor, d_o, o, q, k, v, raw, lse):
    rows, hw = q.shape
    return call(
        attend_back_kernel,
        [((rows, 3 * hw), BF)] + [((2, 2, hw, 512), BF)] * 2,
        places, tokens, factor, d_o, o, q, k, v, raw, lse, smem=1,
        scratch=[pltpu.VMEM((hw, rows), BF), pltpu.VMEM((8, rows), F32), pltpu.VMEM((rows, hw), F32),
                 pltpu.VMEM((rows, hw), F32), pltpu.VMEM((8, hw), F32),
                 pltpu.VMEM((tokens.shape[1] - 128, 3 * hw), F32)],
        vmem=32,
    )


def group_rows(w_ref, group, hw, width):
    return w_ref[pl.ds(pl.multiple_of(group * hw, 16), hw), :width]


def out_kernel(place_ref, h0, h1, h2, h3, w_ref, own_ref, sib_ref):
    tok, width = own_ref.shape
    hw = h0.shape[1]
    total = sum(mm(h[...], group_rows(w_ref, place_ref[0] ^ d, hw, width)) for d, h in enumerate((h0, h1, h2, h3)))
    own_ref[...] = total[:tok]
    sib_ref[...] = total[tok:].astype(BF)


def norm_kernel(x_ref, own_ref, got_ref, x2_ref, n_ref):
    x2 = x_ref[...].astype(F32) + own_ref[...] + got_ref[...].astype(F32)
    x2_ref[...] = x2
    n_ref[...] = (x2 * lax.rsqrt(jnp.mean(x2 * x2, axis=-1, keepdims=True) + norm_eps)).astype(BF)


def pick_columns(rows, core, own):
    q = rows.shape[1] // 4
    odd = core if own else 1 - core
    parts = [jnp.where(odd == 1, rows[:, (2 * b + 1) * q : (2 * b + 2) * q], rows[:, 2 * b * q : (2 * b + 1) * q])
             for b in range(2)]
    return jnp.concatenate(parts, axis=1)


def mlp_kernel(place_ref, n_own_ref, n_sib_ref, cot_own_ref, cot_sib_ref, up_own_ref, up_sib_ref, w_ref, dn_ref,
               act_ref, pre_ref, cols_ref, out_own_ref, out_sib_ref, d_own_ref, d_sib_ref):
    tok, width = n_own_ref.shape
    half = width // 2
    core = place_ref[4]
    n_pair = jnp.concatenate([n_own_ref[...], n_sib_ref[...]], axis=0).astype(F32)
    cols_ref[:, :half] = pick_columns(n_pair, core, True).astype(BF)
    cols_ref[:, half:] = pick_columns(n_pair, core, False).astype(BF)
    biases = w_ref[:, width : width + 128].astype(F32).T
    u = mm(cols_ref[:, :half], up_own_ref[...]) + mm(cols_ref[:, half:], up_sib_ref[...]) + biases[0:1]
    sig = jax.nn.sigmoid(u)
    act_ref[...] = (u * sig).astype(BF)
    slope = sig * (1.0 + u * (1.0 - sig))
    pre_ref[:tok] = (mm(cot_own_ref[...], dn_ref[...], 1, 1) * slope[:tok]).astype(BF)
    pre_ref[tok:] = (mm(cot_sib_ref[...], dn_ref[...], 1, 1) * slope[tok:]).astype(BF)
    d_own = mm(pre_ref[...], up_own_ref[...], 1, 1)
    d_sib = mm(pre_ref[...], up_sib_ref[...], 1, 1)
    d_n = interleave(core, d_own, d_sib)
    d_own_ref[...] = d_n[:tok]
    d_sib_ref[...] = d_n[tok:].astype(BF)
    bias = interleave(core, biases[1:2], jnp.zeros_like(biases[1:2]))
    out = mm(act_ref[...], dn_ref[...]) + bias
    out_own_ref[...] = out[:tok]
    out_sib_ref[...] = out[tok:].astype(BF)


def interleave(core, own, sib):
    q = own.shape[1] // 2
    blocks = []
    for b in range(2):
        a, o = own[:, b * q : (b + 1) * q], sib[:, b * q : (b + 1) * q]
        blocks += [jnp.where(core == 1, o, a), jnp.where(core == 1, a, o)]
    return jnp.concatenate(blocks, axis=1)


def norm_back_kernel(x2_ref, cot_ref, own_ref, got_ref, out_own_ref, out_got_ref, d_ref, low_ref, out_ref):
    x2 = x2_ref[...]
    out_ref[...] = (x2 + out_own_ref[...] + out_got_ref[...].astype(F32)).astype(BF)
    inverse = lax.rsqrt(jnp.mean(x2 * x2, axis=-1, keepdims=True) + norm_eps)
    normed = x2 * inverse
    d_n = own_ref[...] + got_ref[...].astype(F32)
    d_x = cot_ref[...].astype(F32) + inverse * (d_n - normed * jnp.mean(d_n * normed, axis=-1, keepdims=True))
    d_ref[...] = d_x
    low_ref[...] = d_x.astype(BF)


def attn_grad_kernel(place_ref, own_ref, sib_ref, w_ref, *outs):
    tok, width = own_ref.shape
    hw = outs[0].shape[1]
    for d, out in enumerate(outs):
        w = group_rows(w_ref, place_ref[0] ^ d, hw, width)
        out[:tok, :] = mm(own_ref[...], w, 1, 1).astype(BF)
        out[tok:, :] = mm(sib_ref[...], w, 1, 1).astype(BF)


def deal(place_ref, blocks_ref, keep_ref, send_ref):
    core, y, x = place_ref[4], place_ref[1], place_ref[2]
    for far, out in enumerate((keep_ref, send_ref)):
        for i in range(8):
            near, z = i // 4, i % 4
            bx = x ^ jnp.where(core == 1, near, far)
            by = y ^ jnp.where(core == 1, far, near)
            out[i] = blocks_ref[bx * 8 + z * 2 + by].astype(BF)


def z_deal_kernel(place_ref, keep_ref, got_ref, near_ref, out_ref, send_ref):
    z, near = place_ref[3], 2
    for d, (out, at) in enumerate(((out_ref, 0), (out_ref, 1), (send_ref, 0), (send_ref, 1))):
        i = z ^ (0, near, 3 - near, 3)[d]
        out[at] = (keep_ref[i].astype(F32) + got_ref[i].astype(F32) + near_ref[i].astype(F32)).astype(BF)


def corner_kernel(keep_ref, got_ref, out_ref):
    n = out_ref.shape[0]
    out_ref[...] = (keep_ref[n:].astype(F32) + got_ref[n:].astype(F32)).astype(BF)


def mlp_grad_kernel(place_ref, cols_ref, pre_ref, act_ref, cot_own_ref, cot_sib_ref, keep_ref, send_ref, g_ref):
    tok, width = cot_own_ref.shape
    half = width // 2
    shard = g_ref.shape[1]
    core = place_ref[4]
    cot = jnp.concatenate([cot_own_ref[...], cot_sib_ref[...]], axis=0)
    s_up = jnp.sum(pre_ref[...].astype(F32), axis=0, keepdims=True)
    s_dn = pick_columns(jnp.sum(cot.astype(F32), axis=0, keepdims=True), core, True)
    biases = jnp.concatenate([s_up, s_dn, jnp.zeros((126, half), F32)], axis=0).T
    act_t = act_ref[...].astype(F32).T.astype(BF)
    own_t = cols_ref[:, :half].astype(F32).T.astype(BF)
    sib_t = cols_ref[:, half:].astype(F32).T.astype(BF)
    step = 4 * shard
    for i in range(half // step):
        rows = slice(i * step, (i + 1) * step)
        g = mm(act_t[rows], cot)
        own, sib = mm(own_t[rows], pre_ref[...]), mm(sib_t[rows], pre_ref[...])
        for b in range(4):
            at = slice(b * shard, (b + 1) * shard)
            g_ref[4 * i + b, :, :width] = g[at]
            g_ref[4 * i + b, :, width : width + 128] = biases[i * step + b * shard : i * step + (b + 1) * shard]
            g_ref[4 * i + b, :, width + 128 : width + 128 + half] = own[at]
            g_ref[4 * i + b, :, width + 128 + half :] = sib[at]
    deal(place_ref, g_ref, keep_ref, send_ref)


def out_grad_kernel(place_ref, h0, h1, h2, h3, own_ref, sib_ref, keep_ref, send_ref, g_ref):
    shard = g_ref.shape[1]
    d_branch = jnp.concatenate([own_ref[...], sib_ref[...]], axis=0)
    for d, h_ref in enumerate((h0, h1, h2, h3)):
        g = mm(h_ref[...].astype(F32).T.astype(BF), d_branch)
        for b in range(4):
            g_ref[(place_ref[0] ^ d) * 4 + b] = g[b * shard : (b + 1) * shard]
    deal(place_ref, g_ref, keep_ref, send_ref)


def column(row):
    n = row.shape[1]
    same = lax.broadcasted_iota(jnp.int32, (n, n), 0) == lax.broadcasted_iota(jnp.int32, (n, n), 1)
    return jnp.sum(jnp.where(same, row, 0.0), axis=1, keepdims=True)


def row_of(col):
    n = col.shape[0]
    same = lax.broadcasted_iota(jnp.int32, (n, n), 0) == lax.broadcasted_iota(jnp.int32, (n, n), 1)
    return jnp.sum(jnp.where(same, col, 0.0), axis=0, keepdims=True)


def prep_kernel(place_ref, g1_ref, g2_ref, bu_ref, bd_ref, wq_ref, wo_ref, wu_ref, wd_ref, keep_ref, send_ref, pay_ref, dn_ref):
    shard, width = wo_ref.shape
    hw = 2 * HEAD_DIM
    core = place_ref[4]
    col = lambda ref: column(ref[...].astype(F32))
    wq = wq_ref[...].astype(F32) * col(g1_ref)
    for g in range(4):
        for t in range(3):
            base = t * width + (g // 2) * 4 * hw + (g % 2) * hw
            a, b = wq[:, base : base + hw], wq[:, base + 2 * hw : base + 3 * hw]
            to = slice(t * hw, (t + 1) * hw)
            keep_ref[g ^ place_ref[0], :, to] = jnp.where(core == 1, b, a).astype(BF)
            send_ref[g ^ place_ref[0], :, to] = jnp.where(core == 1, a, b).astype(BF)
    pay_ref[0, :, :width] = wo_ref[...]
    lane = lax.broadcasted_iota(jnp.int32, (shard, 128), 1)
    extra = jnp.where(lane == 0, col(bu_ref), jnp.where(lane == 1, col(bd_ref), 0.0))
    pay_ref[0, :, width : width + 128] = extra.astype(BF)
    dn_ref[0] = wd_ref[...]
    pay_ref[0, :, width + 128 :] = (wu_ref[...].astype(F32) * col(g2_ref)).astype(BF)


def stack_kernel(*refs):
    *parts, out_ref, sems = refs
    start, copies = 0, []
    for i, part in enumerate(parts):
        copies.append(pltpu.make_async_copy(part, out_ref.at[pl.ds(start, part.shape[0])], sems.at[i]))
        start += part.shape[0]
    for copy in copies:
        copy.start()
    for copy in copies:
        copy.wait()


def stack(*parts):
    lengths = sum(p.shape[0] for p in parts)
    return call(stack_kernel, [((lengths,) + parts[0].shape[1:], BF)], *parts, hbm=tuple(range(len(parts))),
                scratch=[pltpu.SemaphoreType.DMA((len(parts),))])[0]


def z_slot(place_ref, bz):
    d = bz ^ place_ref[3]
    return jnp.where(d == 0, 0, jnp.where(d == 3, 3, jnp.where(d == 2, 1, 2)))


def assemble_kernel(place_ref, a_ref, b_ref, c_ref, d_ref, w_ref, own_ref, send_ref, grid_ref, sems):
    core = place_ref[4]
    xy = place_ref[2] * 2 + place_ref[1]
    near = jnp.where(core == 1, 2, 1)
    copies = [pltpu.make_async_copy(ref, grid_ref.at[xy ^ d], sems.at[i])
              for i, (ref, d) in enumerate(((a_ref, 0), (b_ref, near), (c_ref, 3 - near), (d_ref, 3)))]
    for copy in copies:
        copy.start()
    for copy in copies:
        copy.wait()
    rest = w_ref.shape[1]
    shard = grid_ref.shape[2]
    for bz in range(4):
        slot = z_slot(place_ref, bz)
        for bx in range(2):
            rows = jnp.concatenate([grid_ref[2 * bx, slot].astype(F32), grid_ref[2 * bx + 1, slot].astype(F32)], axis=0)
            at = slice((bx * 4 + bz) * 2 * shard, (bx * 4 + bz + 1) * 2 * shard)
            w_ref[at, :] = rows[:, :rest].astype(BF)
            own_ref[at, :] = pick_columns(rows[:, rest:], core, True).astype(BF)
            send_ref[at, :] = pick_columns(rows[:, rest:], core, False).astype(BF)


def assemble_down_kernel(place_ref, a_ref, b_ref, w_ref, grid_ref, sems):
    core = place_ref[4]
    xy = place_ref[2] * 2 + place_ref[1]
    far = jnp.where(core == 1, 2, 1)
    copies = [pltpu.make_async_copy(ref, grid_ref.at[i], sems.at[i]) for i, ref in enumerate((a_ref, b_ref))]
    for copy in copies:
        copy.start()
    for copy in copies:
        copy.wait()
    shard = grid_ref.shape[2]
    for bz in range(4):
        slot = z_slot(place_ref, bz)
        for bx in range(2):
            rows = []
            for by in range(2):
                d = (2 * bx + by) ^ xy
                is_far = jnp.where((d & far) != 0, 1, 0)
                is_near = jnp.where((d & (3 - far)) != 0, 1, 0)
                rows.append(grid_ref[is_far, slot * 2 + is_near].astype(F32))
            at = slice((bx * 4 + bz) * 2 * shard, (bx * 4 + bz + 1) * 2 * shard)
            w_ref[at, :] = jnp.concatenate(rows, axis=0).astype(BF)


def first_norm_kernel(place_ref, x_ref, ids_ref, n_ref):
    tok, width = x_ref.shape
    x = x_ref[...].astype(F32)
    n_ref[:, :width] = (x * lax.rsqrt(jnp.mean(x * x, axis=-1, keepdims=True) + norm_eps)).astype(BF)
    ids = ids_ref[...].astype(F32)
    ids = jnp.where(place_ref[1] == 1, ids[:, tok:], ids[:, :tok])
    n_ref[:, width:] = jnp.broadcast_to(column(ids), (tok, 128)).astype(BF)


def token_grad_kernel(d_ref, w_ref, own_ref, sib_ref):
    tok = own_ref.shape[1]
    for i in range(4):
        d_n = mm(d_ref[2 * i * tok : 2 * (i + 1) * tok, :], w_ref[...], 1, 1)
        own_ref[i] = d_n[:tok].astype(BF)
        sib_ref[i] = d_n[tok:].astype(BF)


def token_deal_kernel(place_ref, a_ref, b_ref, keep_ref, send_ref):
    near = jnp.where(place_ref[4] == 1, 2, 1)
    for d, (out, at) in enumerate(((keep_ref, 0), (keep_ref, 1), (send_ref, 0), (send_ref, 1))):
        i = (0, near, 3 - near, 3)[d]
        out[at] = (a_ref[i].astype(F32) + b_ref[i].astype(F32)).astype(BF)


def last_norm_kernel(x_ref, d_ref, a_ref, b_ref, c_ref, out_ref):
    x = x_ref[...].astype(F32)
    inverse = lax.rsqrt(jnp.mean(x * x, axis=-1, keepdims=True) + norm_eps)
    normed = x * inverse
    d_n = a_ref[0].astype(F32) + b_ref[0].astype(F32) + c_ref[0].astype(F32)
    d_x = d_ref[...] + inverse * (d_n - normed * jnp.mean(d_n * normed, axis=-1, keepdims=True))
    out_ref[...] = d_x.astype(BF)


def qkv_out_kernel(place_ref, g1_ref, g_ref, wq_ref, share_ref, gain_ref, scale_ref):
    width = wq_ref.shape[1] // 3
    hw = 2 * HEAD_DIM
    scale = jnp.zeros((8, 32), F32)
    pieces = {}
    for j in range(4):
        for c in range(2):
            piece = g_ref[j ^ place_ref[0], c ^ place_ref[4]].astype(F32)
            scale = scale + piece[:8, 3 * hw :]
            pieces[(j // 2) * 4 + c * 2 + j % 2] = piece
    for t in range(3):
        part = jnp.concatenate([pieces[g][:, t * hw : (t + 1) * hw] for g in range(8)], axis=1)
        share_ref[:, t * width : (t + 1) * width] = part
    gain_ref[...] = row_of(jnp.sum(share_ref[...] * wq_ref[...].astype(F32), axis=1, keepdims=True))
    share_ref[...] = share_ref[...] * column(g1_ref[...].astype(F32))
    scale_ref[...] = scale


def last_sum(keep_ref, got_ref, near_ref):
    return keep_ref[0].astype(F32) + got_ref[0].astype(F32) + near_ref[0].astype(F32)


def up_kernel(keep_ref, got_ref, near_ref, out_ref):
    out_ref[...] = last_sum(keep_ref, got_ref, near_ref)[:, -out_ref.shape[1] :].astype(BF)


def rest_out_kernel(place_ref, g2_ref, a0, a1, a2, up_ref, b0, b1, b2, wu_ref,
                    out_ref, share_ref, dn_ref, gain_ref, bu_ref, bd_ref):
    width = out_ref.shape[1]
    half = width // 2
    mine = last_sum(a0, a1, a2)
    out_ref[...] = last_sum(b0, b1, b2)
    up = interleave(place_ref[4], mine[:, width + 128 : width + 128 + half], up_ref[...].astype(F32))
    share_ref[...] = up * column(g2_ref[...].astype(F32))
    gain_ref[...] = row_of(jnp.sum(up * wu_ref[...].astype(F32), axis=1, keepdims=True))
    dn_ref[...] = mine[:, :width]
    bu_ref[...] = row_of(mine[:, width : width + 1])
    bd_ref[...] = row_of(mine[:, width + 1 : width + 2])


def shard_kernel(place_ref, keep_ref, got_ref, near_ref, own_ref, send_ref):
    shard = own_ref.shape[1]
    core = place_ref[4]
    for s, out in enumerate((own_ref, send_ref)):
        c = core ^ s
        total = keep_ref[0, c].astype(F32) + got_ref[0, c].astype(F32) + near_ref[0, c].astype(F32)
        for g in range(4):
            out[g ^ place_ref[0]] = total[g * shard : (g + 1) * shard].astype(BF)


def flip(array, mask_even, mask_odd):
    pairs = [(i, i ^ (mask_odd if i & BIT_C else mask_even)) for i in range(32)]
    return lax.ppermute(array, AXES, pairs)


def flip_core(array):
    return flip(array, BIT_C, BIT_C)


def turn(array):
    def other(i):
        c, z1 = (i // BIT_C) & 1, (i // BIT_Z1) & 1
        return (i & ~(BIT_C | BIT_Z1)) | (z1 * BIT_C) | (c * BIT_Z1)
    return lax.ppermute(array, AXES, [(i, other(i)) for i in range(32)])


def dot(a, b, dims):
    return lax.dot_general(a, b, (dims, ((), ())), preferred_element_type=F32)


def place(blocks, index_of, axis=0):
    out = jnp.zeros((len(blocks),) + blocks[0].shape, blocks[0].dtype)
    for d, block in enumerate(blocks):
        out = lax.dynamic_update_index_in_dim(out, block, index_of(d), 0)
    return out


def after(array, *others):
    return lax.optimization_barrier((array,) + others)[0]


def square_shards(block_input, block_ids, w_qkv, w_out, w_up, w_down, gain_attn, gain_mlp,
                  bias_up, bias_down, query_scale, out_cotangent):
    width = block_input.shape[2]
    tok = block_input.shape[1]
    shard = w_qkv.shape[0]
    half = width // 2
    hw = 2 * HEAD_DIM
    bit_x, bit_c, bit_z1, bit_z0, bit_y = [lax.axis_index(name) for name in AXES]
    core = bit_c == 1
    j = bit_z0 * 2 + bit_y
    places = jnp.stack([j, bit_y, bit_x, bit_z1 * 2 + bit_z0, bit_c, bit_z1]).astype(jnp.int32)
    rows_f, rows_b = ((tok, width), F32), ((tok, width), BF)
    by_core = lambda a, b: jnp.where(core, b, a)
    sems = lambda n: pltpu.SemaphoreType.DMA((n,))

    row = lambda v: v.reshape(1, shard)
    keep, send, pay, pay_dn = call(
        prep_kernel, [((4, shard, 3 * hw), BF)] * 2 + [((1, shard, 2 * width + 128), BF), ((1, shard, width), BF)],
        places, row(gain_attn), row(gain_mlp), row(bias_up), row(bias_down), w_qkv, w_out, w_up, w_down, smem=1, vmem=56)

    x_low = turn(after(block_input[0], pay))
    ids_low = turn(after(block_ids, pay))
    sib = flip_core(send)
    p1 = flip(pay, BIT_Z1, BIT_Z1)

    sib = after(sib, ids_low)
    cuts = [jnp.stack([keep[d], sib[d]]) for d in range(4)]
    got = [flip(cuts[d], d, d) for d in (1, 2, 3)]

    (n_msg,) = call(first_norm_kernel, [((tok, width + 128), BF)], places, x_low, ids_low, smem=1)
    p1 = after(p1, n_msg)
    p_two = stack(pay, p1)
    p2 = flip(p_two, BIT_Z0, BIT_Z0)
    r1 = flip(n_msg, BIT_Y, BIT_Z0)
    got[0] = after(got[0], p_two)
    grid = jnp.zeros((2, 4, shard, 3 * hw), BF)
    for d, pair in enumerate([cuts[0]] + got):
        for o in range(2):
            grid = lax.dynamic_update_slice(grid, pair[o][None, None], (bit_c ^ o, j ^ d, 0, 0))
    grid = grid.reshape(2, 4 * shard, 3 * hw)
    a_z = flip(grid, BIT_Z1, BIT_Z1)
    a_x = flip(grid, BIT_X, BIT_X)
    q1 = flip(after(pay_dn, grid), BIT_X, BIT_Y)
    r1 = after(r1, grid)
    n_two = stack(n_msg, r1)
    r2 = flip(n_two, BIT_Z0, BIT_Y)
    q1 = after(q1, n_two)
    q_two = stack(pay_dn, q1)
    p2 = after(p2, q_two)
    p_four = stack(p_two, p2)
    p3 = flip(p_four, BIT_Y, BIT_X)
    a_x = after(a_x, p_four)
    a_z = after(a_z, a_x)
    a_xz = flip(a_z, BIT_X, BIT_X)
    p4 = flip(after(p_four, a_z), BIT_X, BIT_Y)
    p3 = after(p3, a_z)
    p5 = flip(p3, BIT_X, BIT_Y)
    q2 = flip(after(q_two, p3), BIT_Z1, BIT_Z1)
    m01 = flip_core(after(n_two, p3))
    r2 = after(r2, p3)
    m2 = flip_core(r2)
    m01 = after(m01, r2)
    m2 = after(m2, m01)
    q2 = after(q2, m2)
    q_four = stack(q_two, q2)
    q3 = flip(q_four, BIT_Z0, BIT_Z0)
    a_xz = after(a_xz, q_four)
    k_now = bit_x * 2 + bit_z1
    wq_full = place([grid, a_z, a_x, a_xz], lambda d: k_now ^ d)
    wq_full = wq_full.reshape(2, 2, 2, 4 * shard, 3 * hw).transpose(0, 2, 1, 3, 4).reshape(width, 3 * hw)
    by_y = by_core(r1, r2[:tok]), by_core(m2[:tok], m01[tok:])
    by_z = by_core(r2[:tok], r1), by_core(m01[tok:], m2[:tok])
    tokens = jnp.concatenate([n_msg, m01[:tok], *by_y, *by_z, r2[tok:], m2[tok:]], axis=0)

    base = scale_base / math.sqrt(HEAD_DIM)
    factor = jnp.stack([jnp.tile(base * jax.nn.softplus(query_scale), 2), jnp.tile(base * jax.nn.sigmoid(query_scale), 2)])
    attn, q_h, k_h, v_h, q_raw, lse = attend(tokens, wq_full, factor)
    cot_own = turn(after(out_cotangent[0], attn))
    p4 = after(p4, attn)
    q3 = after(q3, p4)
    q_eight = stack(q_four, q3)
    heads = [attn[0]] + [flip(after(attn[d], q_eight), d, d) for d in (1, 2, 3)]
    p5 = after(p5, q_eight)
    q4 = flip(after(q_eight, p5), BIT_Y, BIT_X)
    heads[1] = after(heads[1], p5)
    cot_own = after(cot_own, *heads[1:])
    cot_sib = flip_core(cot_own)
    w, up_own, up_send = call(
        assemble_kernel, [((half, width + 128), BF), ((half, half), BF), ((half, half), BF)],
        places, p_four, p3, p4, after(p5, cot_own), smem=1, vmem=24, hbm=(1, 2, 3, 4),
        scratch=[pltpu.VMEM((4, 4) + pay.shape[1:], BF), sems(4)])
    up_sib = flip_core(up_send)

    part, part_sib = call(out_kernel, [rows_f, rows_b], places, *heads, w, smem=1)
    x2, n_two = call(norm_kernel, [rows_f, rows_b], x_low, part, flip_core(part_sib), vmem=8)
    q4 = after(q4, n_two)
    (dn,) = call(
        assemble_down_kernel, [((half, width), BF)], places, q_eight, q4, smem=1, vmem=16, hbm=(1, 2),
        scratch=[pltpu.VMEM((2, 8) + pay_dn.shape[1:], BF), sems(2)])
    act, d_pre, n_cols, out_own, out_sib, d_own, d_sib = call(
        mlp_kernel,
        [((2 * tok, half), BF), ((2 * tok, half), BF), ((2 * tok, width), BF), rows_f, rows_b, rows_f, rows_b],
        places, n_two, flip_core(n_two), cot_own, cot_sib, up_own, up_sib, w, dn, smem=1, vmem=24)
    d_x2, d_branch, out = call(
        norm_back_kernel, [rows_f, rows_b, rows_b], x2, cot_own, d_own, flip_core(d_sib), out_own, flip_core(out_sib), vmem=8)
    branch_sib = flip_core(d_branch)
    wide = 2 * width + 128
    pieces = lambda columns: [((8, shard, columns), BF)] * 2
    d_attn = call(attn_grad_kernel, [((2 * tok, hw), BF)] * 4, places, d_branch, branch_sib, w, smem=1)
    moved = [flip(d_attn[d], d, d) for d in (1, 2, 3)]
    a_keep, a_send = call(
        mlp_grad_kernel, pieces(wide), places, n_cols, d_pre, act, cot_own, after(cot_sib, d_attn[3]),
        smem=1, vmem=24, scratch=[pltpu.VMEM((16, shard, wide), F32)])
    b_keep, b_send = call(
        out_grad_kernel, pieces(width), places, *heads, after(d_branch, a_send), branch_sib,
        smem=1, scratch=[pltpu.VMEM((16, shard, width), F32)])

    a_got = flip(after(a_send, moved[0]), BIT_X, BIT_Y)
    b_got = flip(after(b_send, moved[2]), BIT_X, BIT_Y)

    def corner(keep, got):
        return call(corner_kernel, [((keep.shape[0] // 2,) + keep.shape[1:], BF)], keep, got)[0]

    def z_deal(keep, got, near):
        return call(z_deal_kernel, [((2,) + keep.shape[1:], BF)] * 2, places, keep, got, near, smem=1)

    moved[2] = after(moved[2], b_send)
    d_o = jnp.concatenate([d_attn[0], *moved], axis=0)
    d_qkv, g_keep, g_send = attend_back(places, tokens, factor, d_o, attn, q_h, k_h, v_h, q_raw, lse)
    g_got = flip(g_send, BIT_Z1, BIT_X)
    d_n, d_n_sib = call(token_grad_kernel, [((4, tok, width), BF)] * 2, after(d_qkv, g_send), wq_full)
    from_sib = flip_core(d_n_sib)

    a_got = after(a_got, d_n)
    a_near = flip(corner(a_keep, a_got), BIT_Y, BIT_X)
    from_sib = after(from_sib, a_got)
    t_keep, t_send = call(token_deal_kernel, [((2, tok, width), BF)] * 2, places, d_n, from_sib, smem=1)
    t_got = flip(t_send, BIT_Z0, BIT_Y)
    b_got = after(b_got, t_send)
    b_near = flip(corner(b_keep, b_got), BIT_Y, BIT_X)
    g_got = after(g_got, b_got)
    g_near = flip(corner(g_keep, g_got), BIT_X, BIT_Z1)
    t_got = after(t_got, g_got)
    t_near = flip(corner(t_keep, t_got), BIT_Y, BIT_Z0)
    a_near = after(a_near, t_got)
    a_keep, a_send = z_deal(a_keep, a_got, a_near)
    a_got = flip(a_send, BIT_Z0, BIT_Z0)
    g_near = after(g_near, a_send)
    out = turn(after(out, g_near))
    g_own, g_sib = call(shard_kernel, [((4, shard, 512), BF)] * 2, places, g_keep, g_got, g_near, smem=1)
    g_sib = flip_core(g_sib)
    b_near = after(b_near, g_own)
    b_keep, b_send = z_deal(b_keep, b_got, b_near)
    b_got = flip(b_send, BIT_Z0, BIT_Z0)
    t_near = after(t_near, b_send)
    (grad_x,) = call(last_norm_kernel, [rows_b], x_low, d_x2, t_keep, t_got, t_near)
    g_sib = after(g_sib, grad_x)
    grad_x = turn(grad_x)
    rel = [jnp.stack([g_own[d], g_sib[d]]) for d in range(4)]
    rel = [rel[0]] + [flip(rel[d], d, d) for d in (1, 2, 3)]
    a_got = after(a_got, rel[0])
    a_near = flip(corner(a_keep, a_got), BIT_Z1, BIT_Z1)
    b_got = after(b_got, a_got)
    b_near = flip(corner(b_keep, b_got), BIT_Z1, BIT_Z1)
    rel[1] = after(rel[1], b_got)
    share_qkv, grad_gain_one, scale = call(
        qkv_out_kernel, [((shard, 3 * width), F32), ((1, shard), F32), ((8, 32), F32)],
        places, row(gain_attn), jnp.stack(rel), w_qkv, smem=1)
    scale_total = scale[:3].reshape(96)[:HEAD_DIM]
    a_near = after(a_near, share_qkv)
    (up_other,) = call(up_kernel, [((shard, half), BF)], a_keep, a_got, a_near)
    up_other = flip_core(up_other)
    share_out, share_up, share_down, grad_gain_two, grad_bup, grad_bdown = call(
        rest_out_kernel,
        [((shard, width), F32)] * 3 + [((1, shard), F32)] * 3,
        places, row(gain_mlp), a_keep, a_got, a_near, up_other, b_keep, b_got, b_near, w_up, smem=1)
    vector = lambda v: v.reshape(shard)
    return (out[None], grad_x.astype(F32)[None], share_qkv, share_out, share_up, share_down,
            vector(grad_gain_one), vector(grad_gain_two), vector(grad_bup), vector(grad_bdown), scale_total)


def solution(mesh):
    if dict(mesh.shape) == {"dp": 4, "blk": 4, "head": 2}:
        mesh = Mesh(mesh.devices.reshape(2, 2, 2, 2, 2), AXES)
        seqs, tokens, heads, body = ("x", "c"), ("z1", "z0"), ("y",), square_shards
    else:
        seqs, tokens, heads, body = ("dp",), ("blk",), ("head",), shards
    rows = P(seqs, tokens + heads, None)
    weight = P(seqs + tokens + heads, None)
    vector = P(seqs + tokens + heads)
    return jax.shard_map(
        body,
        mesh=mesh,
        in_specs=(rows, P(seqs, tokens)) + (weight,) * 4 + (vector,) * 4 + (P(), rows),
        out_specs=(rows, rows) + (weight,) * 4 + (vector,) * 4 + (P(),),
        check_vma=False,
    )
```
